512 devices in a mesh: row: 32 (over y, x), help: 16 (over z, core).
Axes of the slice: x: 4, y: 8, z: 8, core: 2. Of those that a mesh axis runs over, the one named last changes fastest.
Arguments:
- factor_inv: bfloat16 [1024, 1024, 1024], P(('row', 'help'))
- b_rows: int32 [1024, 512], P(('row', 'help')), may hold values from 0 to 1023
- b_coef: float32 [1024, 512], P(('row', 'help')), may hold values from -1 to 1
- b_count: int32 [1024], P(('row', 'help')), may hold values from 128 to 512
- refined: int32 [32, 8], P('row'), may hold values from 0 to 31, as said below
- modes: float32 [1024, 6, 1024], P(('row', 'help')), may hold values from -6 to 6
- owner: int32 [1024, 512], P(('row', 'help')), may hold values from 0 to 511
Outputs:
- dual_blocks: bfloat16 [256, 512, 512], P('row', 'help')
- coarse: float32 [6144, 512], P(None, 'row')
The draws below stay inside these ranges and needn't reach their ends.
Inputs may be any that keep to these rules, and one draw needn't show every extreme that they name: Each row of refined holds 8 numbers l of different devices' ranges, device d's range being 2 * d to 2 * d + 1, so no device holds more than one listed subdomain.
All inputs are finite; a program needn't handle non-finite values.
Results may differ from the reference program's by a relative error of at most 0.0065.
Values may be sent and summed in bfloat16 or wider, within the bound.
A program may use at most 64 MiB of HBM per device.

```python
import jax
import jax.numpy as jnp
from jax import lax

N = 1024
M = 512
SUB = 2
MODES = 6
LAM_DEV = 16
S = 1024
LIST = 8
NLAM = 512
N_ROW = 32
N_HELP = 16


def draw_factor_inv(key, part):
    key = jax.random.fold_in(key, 11)
    first, second = jax.random.split(key)
    noise = jax.random.normal(first, (S, N, N), jnp.float32)
    diagonal = jnp.exp(jax.random.uniform(second, (S, N), jnp.float32, jnp.log(0.5), jnp.log(2.0)))
    rows_at = lax.broadcasted_iota(jnp.int32, (N, N), 0)
    cols_at = lax.broadcasted_iota(jnp.int32, (N, N), 1)
    lower = (rows_at > cols_at).astype(jnp.float32)
    same = (rows_at == cols_at).astype(jnp.float32)
    matrix = noise * (0.6 / jnp.sqrt(jnp.float32(N))) * lower[None] + diagonal[:, :, None] * same[None]
    return matrix.astype(jnp.bfloat16)


def draw_refined(key, part):
    key = jax.random.fold_in(key, 23)
    group_keys = jax.random.split(key, N_ROW)
    group_ids = jnp.arange(N_ROW, dtype=jnp.int32)

    def one_group(group_key, group_id):
        pick_key, slot_key = jax.random.split(group_key)
        order = jax.random.permutation(pick_key, N_HELP).astype(jnp.int32)
        target = jnp.where(group_id == 0, 0, jnp.where(group_id == N_ROW - 1, N_HELP - 1, order[0])).astype(jnp.int32)
        shifted = ((order - order[0] + target) % N_HELP).astype(jnp.int32)
        devices = shifted[:LIST]
        slot_pick = jax.random.randint(slot_key, (LIST,), 0, SUB).astype(jnp.int32)
        first_slot = jnp.where(group_id == 0, 0, jnp.where(group_id == N_ROW - 1, SUB - 1, slot_pick[0])).astype(jnp.int32)
        slot_pick = slot_pick.at[0].set(first_slot)
        return (devices * SUB + slot_pick).astype(jnp.int32)
    return jax.vmap(one_group)(group_keys, group_ids)


def touch_ends(result, rng, least, largest):
    shape = result.shape
    place = [jax.random.randint(jax.random.fold_in(rng, axis), (), 0, shape[axis]) for axis in range(len(shape))]
    result = result.at[tuple(place)].set(least)
    longest = shape.index(max(shape))
    place[longest] = (place[longest] + 1) % shape[longest]
    return result.at[tuple(place)].set(largest)


def level_of(key, extent, pieces, smallest, largest):
    factor_of = 1.0
    for position, parts in pieces:
        steps = jax.random.uniform(jax.random.fold_in(jax.random.fold_in(key, 6), position), (parts,), jnp.float32, smallest / len(pieces), largest / len(pieces))
        factor_of = factor_of * jnp.repeat(jnp.exp(steps), extent[position] // parts).reshape((-1,) + (1,) * (len(extent) - 1 - position))
    return factor_of


def centred(key, dims, scale, most, cuts=(), kind=jnp.bfloat16):
    array = jax.random.normal(key, dims, jnp.float32) * scale
    if len(cuts) > 0:
        array = level_of(key, dims, cuts, -0.22, 0.18) * array
    return jnp.clip(array, min=-most, max=most).astype(kind)


def setup_inputs(seed: int = 0) -> dict:
    streams_of = jax.random.split(jax.random.key(seed), 8)
    factor_inv = draw_factor_inv(jax.random.fold_in(streams_of[7], 71), 0)
    b_rows = touch_ends(jax.random.randint(streams_of[1], (S, M), 0, N), jax.random.fold_in(streams_of[1], 1), 0, N - 1).astype(jnp.int32)
    b_coef = jnp.clip(jax.random.uniform(streams_of[2], (S, M), jnp.float32, -1.0, 1.0) * level_of(streams_of[2], (S, M), ((0, 512),), -0.4, 0.0), -1.0, 1.0)
    b_count = touch_ends(jax.random.randint(streams_of[3], (S,), M // 4, M + 1), jax.random.fold_in(streams_of[3], 1), M // 4, M).astype(jnp.int32)
    refined = draw_refined(jax.random.fold_in(streams_of[7], 71), 0)
    modes = centred(streams_of[5], (S, MODES, N), 1.0, 6.0, ((0, 512),), jnp.float32)
    owner = touch_ends(jax.random.randint(streams_of[6], (S, M), 0, NLAM), jax.random.fold_in(streams_of[6], 1), 0, NLAM - 1).astype(jnp.int32)
    return {"factor_inv": factor_inv, "b_rows": b_rows, "b_coef": b_coef, "b_count": b_count, "refined": refined, "modes": modes, "owner": owner}


def panel_weights(b_coef, b_count):
    column = lax.broadcasted_iota(jnp.int32, b_coef.shape, 1)
    return jnp.where(column < b_count[:, None], b_coef, jnp.float32(0.0)).astype(jnp.float32)


def owner_terms(values, owned):
    return jnp.zeros((MODES, LAM_DEV * N_ROW), jnp.float32).at[:, owned].add(values)


def reference(factor_inv, b_rows, b_coef, b_count, refined, modes, owner):
    weights = panel_weights(b_coef, b_count)
    listed = refined.reshape(-1).astype(jnp.int32)

    def assemble(index):
        group = index // LIST
        sub_id = (group * (SUB * N_HELP) + listed[index]).astype(jnp.int32)
        matrix = factor_inv[sub_id]
        picked = jnp.take(matrix, b_rows[sub_id], axis=1).astype(jnp.float32) * weights[sub_id][None, :]
        panel = picked.astype(jnp.bfloat16).astype(jnp.float32)
        gram = lax.dot_general(panel, panel, (((0,), (0,)), ((), ())), preferred_element_type=jnp.float32)
        return gram.astype(jnp.bfloat16)

    dual_blocks = lax.map(assemble, jnp.arange(N_ROW * LIST, dtype=jnp.int32))
    gather_rows = jnp.broadcast_to(b_rows[:, None, :], (modes.shape[0], MODES, M))
    values = jnp.take_along_axis(modes, gather_rows, axis=2) * weights[:, None, :]
    coarse = jax.vmap(owner_terms)(values, owner).reshape(-1, LAM_DEV * N_ROW)
    return dual_blocks, coarse
```

```python
import functools

import jax
import jax.numpy as jnp
from jax import lax
from jax.experimental import pallas as pl
from jax.experimental.pallas import tpu as pltpu
from jax.sharding import PartitionSpec as P

MESH = pl.DeviceIdType.MESH
BF16 = jnp.bfloat16
F32 = jnp.float32
TERM_ROWS = 16
X_TILE = 256
GRAM_TILE = 256
VMEM_LIMIT = 59 * 1024 * 1024


def one_hot(rows, count):
    at = lax.broadcasted_iota(jnp.int32, (count, rows.shape[1]), 0)
    return jnp.where(at == rows, F32(1.0), F32(0.0)).astype(BF16)


def two_parts(x):
    high = x.astype(BF16)
    low = (x - high.astype(F32)).astype(BF16)
    return jnp.concatenate([high, low], axis=0)


def sum_parts(x):
    half = x.shape[0] // 2
    return x[:half] + x[half:]


def assemble_and_send(
    groups, parts, lam_dev,
    count_ref, refined_ref, rows_ref, coef_ref, modes_ref, owner_ref, factor_hbm,
    dual_ref, coarse_ref,
    factor, picker, weight, stacked, panel, gram, term, terms, turned,
    load_sem, send_dual, recv_dual, send_term, recv_term, send_turn, recv_turn, send_pair, recv_pair, keep_sem,
):
    row = lax.axis_index("row")
    part = lax.axis_index("help")
    core = part % 2
    chip = part // 2
    chips = parts // 2
    slots, order, _ = factor_hbm.shape
    width = rows_ref.shape[1]
    modes = modes_ref.shape[0]
    used = slots * modes
    share = width // parts

    loads = []
    for tile in range(order // X_TILE):
        at = pl.ds(tile * X_TILE, X_TILE)
        loads.append(pltpu.make_async_copy(factor_hbm.at[:, at, :], factor[tile], load_sem.at[tile]))
        loads[-1].start()

    barrier = pltpu.get_barrier_semaphore()

    def greet_help(step, _):
        pl.semaphore_signal(barrier, inc=1, device_id=(row, (part + step) % parts), device_id_type=MESH)
        return 0

    def greet_row(step, _):
        pl.semaphore_signal(barrier, inc=1, device_id=((row + step) % groups, part), device_id_type=MESH)
        return 0

    lax.fori_loop(1, parts, greet_help, 0)
    lax.fori_loop(1, groups, greet_row, 0)

    stacked[...] = jnp.zeros_like(stacked)
    column = lax.broadcasted_iota(jnp.int32, (1, width), 1)
    term_row = lax.broadcasted_iota(jnp.int32, (TERM_ROWS, width), 0)
    for slot in range(slots):
        stacked[slot * modes : (slot + 1) * modes, :] = modes_ref[:, slot, :]
        weight[slot] = jnp.where(column < count_ref[slot], coef_ref[slot : slot + 1, :], F32(0.0))
        picker[slot] = one_hot(rows_ref[slot : slot + 1, :], order)
    both = two_parts(stacked[...])
    total = jnp.zeros((TERM_ROWS, groups * lam_dev), F32)
    for slot in range(slots):
        picked = sum_parts(jnp.dot(both, picker[slot], preferred_element_type=F32))
        mine = (term_row >= slot * modes) & (term_row < (slot + 1) * modes)
        values = jnp.where(mine, picked * weight[slot], F32(0.0))
        owned = one_hot(owner_ref[slot : slot + 1, :], groups * lam_dev)
        total += sum_parts(
            lax.dot_general(two_parts(values), owned, (((1,), (1,)), ((), ())), preferred_element_type=F32)
        )
    term[...] = total.astype(BF16)
    terms[chip] = total.astype(BF16)

    pl.semaphore_wait(barrier, parts - 1 + groups - 1)

    def term_copy(step):
        other = (chip + step) % chips
        return pltpu.make_async_remote_copy(
            src_ref=term, dst_ref=terms.at[chip],
            send_sem=send_term.at[step], recv_sem=recv_term.at[step],
            device_id=(row, other * 2 + core), device_id_type=MESH,
        )

    def term_arrival(step):
        other = (chip + chips - step) % chips
        return pltpu.make_async_remote_copy(
            src_ref=term, dst_ref=terms.at[other],
            send_sem=send_term.at[step], recv_sem=recv_term.at[step],
            device_id=(row, other * 2 + core), device_id_type=MESH,
        )

    def start(copy):
        def body(step, _):
            copy(step).start()
            return 0
        return body

    def arrived(copy):
        def body(step, _):
            copy(step).wait_recv()
            return 0
        return body

    def sent(copy):
        def body(step, _):
            copy(step).wait_send()
            return 0
        return body

    lax.fori_loop(1, chips, start(term_copy), 0)

    chosen = jnp.int32(0)
    for entry in range(refined_ref.shape[1]):
        listed = refined_ref[0, entry]
        chosen = jnp.where(listed == part * slots + 1, jnp.int32(1), chosen)
    scale = weight[chosen]
    for tile in range(order // X_TILE):
        loads[tile].wait()
        at = pl.ds(tile * X_TILE, X_TILE)
        picked = jnp.dot(factor[tile][chosen], picker[chosen], preferred_element_type=F32)
        panel[at, :] = (picked * scale).astype(BF16)
    for tile in range(width // GRAM_TILE):
        at = pl.ds(tile * GRAM_TILE, GRAM_TILE)
        gram[at, :] = lax.dot_general(
            panel[:, at], panel[...], (((0,), (0,)), ((), ())), preferred_element_type=F32
        ).astype(BF16)

    def dual_copy(step):
        other = (part + step) % parts
        return pltpu.make_async_remote_copy(
            src_ref=gram.at[pl.ds(other * share, share), :], dst_ref=dual_ref.at[part],
            send_sem=send_dual.at[step], recv_sem=recv_dual.at[step],
            device_id=(row, other), device_id_type=MESH,
        )

    def dual_arrival(step):
        other = (part + parts - step) % parts
        return pltpu.make_async_remote_copy(
            src_ref=gram.at[pl.ds(other * share, share), :], dst_ref=dual_ref.at[other],
            send_sem=send_dual.at[step], recv_sem=recv_dual.at[step],
            device_id=(row, other), device_id_type=MESH,
        )

    lax.fori_loop(1, parts, start(dual_copy), 0)
    keep_dual = pltpu.make_async_copy(
        gram.at[pl.ds(part * share, share), :], dual_ref.at[part], keep_sem.at[0]
    )
    keep_dual.start()

    lax.fori_loop(1, chips, arrived(term_arrival), 0)
    beside = terms[...].reshape(chips * TERM_ROWS, groups * lam_dev)
    turned[...] = jnp.transpose(beside.astype(F32)).astype(BF16)

    def turn_copy(step):
        other = (row + step) % groups
        return pltpu.make_async_remote_copy(
            src_ref=turned.at[pl.ds(other * lam_dev, lam_dev), :], dst_ref=coarse_ref.at[core, row],
            send_sem=send_turn.at[step], recv_sem=recv_turn.at[step],
            device_id=(other, part), device_id_type=MESH,
        )

    def turn_arrival(step):
        other = (row + groups - step) % groups
        return pltpu.make_async_remote_copy(
            src_ref=turned.at[pl.ds(other * lam_dev, lam_dev), :], dst_ref=coarse_ref.at[core, other],
            send_sem=send_turn.at[step], recv_sem=recv_turn.at[step],
            device_id=(other, part), device_id_type=MESH,
        )

    lax.fori_loop(1, groups, start(turn_copy), 0)
    keep_turn = pltpu.make_async_copy(
        turned.at[pl.ds(row * lam_dev, lam_dev), :], coarse_ref.at[core, row], keep_sem.at[1]
    )
    keep_turn.start()
    keep_turn.wait()
    lax.fori_loop(1, groups, arrived(turn_arrival), 0)

    there = chip * 2 + 1 - core
    pair_copy = pltpu.make_async_remote_copy(
        src_ref=coarse_ref.at[core], dst_ref=coarse_ref.at[core],
        send_sem=send_pair, recv_sem=recv_pair,
        device_id=(row, there), device_id_type=MESH,
    )
    pair_arrival = pltpu.make_async_remote_copy(
        src_ref=coarse_ref.at[1 - core], dst_ref=coarse_ref.at[1 - core],
        send_sem=send_pair, recv_sem=recv_pair,
        device_id=(row, there), device_id_type=MESH,
    )
    pair_copy.start()
    pair_arrival.wait_recv()
    keep_dual.wait()
    lax.fori_loop(1, parts, arrived(dual_arrival), 0)
    pair_copy.wait_send()
    lax.fori_loop(1, chips, sent(term_copy), 0)
    lax.fori_loop(1, groups, sent(turn_copy), 0)
    lax.fori_loop(1, parts, sent(dual_copy), 0)


def put_in_order(slots, used, refined_ref, dual_ref, coarse_ref, blocks_ref, out_ref):
    for entry in range(refined_ref.shape[1]):
        blocks_ref[entry] = dual_ref[lax.div(refined_ref[0, entry], slots)]
    cores, groups, lam_dev, lanes = coarse_ref.shape
    per_group = (lanes // TERM_ROWS) * cores * used
    source = lax.broadcasted_iota(jnp.int32, (cores * lanes, 1), 0)
    core, inside = source // lanes, source % lanes
    chip, at = inside // TERM_ROWS, inside % TERM_ROWS
    target = jnp.where(at < used, (chip * cores + core) * used + at, -512)
    lane = lax.broadcasted_iota(jnp.int32, (cores * lanes, 2 * lanes), 1)
    beside = jnp.concatenate(
        [coarse_ref[c].reshape(groups * lam_dev, lanes) for c in range(cores)], axis=1
    )
    shift = per_group - lanes
    even = jnp.dot(beside, jnp.where(lane == target, F32(1.0), F32(0.0)).astype(BF16), preferred_element_type=F32)
    odd = jnp.dot(beside, jnp.where(lane == target + shift, F32(1.0), F32(0.0)).astype(BF16), preferred_element_type=F32)
    for pair in range(groups // 2):
        first = even[2 * pair * lam_dev : (2 * pair + 1) * lam_dev]
        second = odd[(2 * pair + 1) * lam_dev : (2 * pair + 2) * lam_dev]
        base = pair * 3 * lanes
        out_ref[:, base : base + lanes] = first[:, :lanes]
        out_ref[:, base + lanes : base + 2 * lanes] = first[:, lanes:] + second[:, :lanes]
        out_ref[:, base + 2 * lanes : base + 3 * lanes] = second[:, lanes:]


def on_device(groups, parts, factor_inv, b_rows, b_coef, b_count, refined, modes, owner, lam_dev):
    slots, order, _ = factor_inv.shape
    width = b_rows.shape[1]
    mode_count = modes.shape[1]
    share = width // parts
    chips = parts // 2
    lanes = chips * TERM_ROWS
    lam = groups * lam_dev
    vmem = pl.BlockSpec(memory_space=pltpu.VMEM)
    smem = pl.BlockSpec(memory_space=pltpu.SMEM)
    anywhere = pl.BlockSpec(memory_space=pl.ANY)
    dual, coarse = pl.pallas_call(
        functools.partial(assemble_and_send, groups, parts, lam_dev),
        out_shape=(
            jax.ShapeDtypeStruct((parts, share, width), BF16),
            jax.ShapeDtypeStruct((2, groups, lam_dev, lanes), BF16),
        ),
        in_specs=[smem, smem, vmem, vmem, vmem, vmem, anywhere],
        out_specs=(anywhere, anywhere),
        scratch_shapes=[
            [pltpu.VMEM((slots, X_TILE, order), BF16) for _ in range(order // X_TILE)],
            pltpu.VMEM((slots, order, width), BF16),
            pltpu.VMEM((slots, 1, width), F32),
            pltpu.VMEM((TERM_ROWS, order), F32),
            pltpu.VMEM((order, width), BF16),
            pltpu.VMEM((width, width), BF16),
            pltpu.VMEM((TERM_ROWS, lam), BF16),
            pltpu.VMEM((chips, TERM_ROWS, lam), BF16),
            pltpu.VMEM((lam, lanes), BF16),
            pltpu.SemaphoreType.DMA((order // X_TILE,)),
            pltpu.SemaphoreType.DMA((parts,)),
            pltpu.SemaphoreType.DMA((parts,)),
            pltpu.SemaphoreType.DMA((chips,)),
            pltpu.SemaphoreType.DMA((chips,)),
            pltpu.SemaphoreType.DMA((groups,)),
            pltpu.SemaphoreType.DMA((groups,)),
            pltpu.SemaphoreType.DMA,
            pltpu.SemaphoreType.DMA,
            pltpu.SemaphoreType.DMA((2,)),
        ],
        compiler_params=pltpu.CompilerParams(
            collective_id=0, has_side_effects=True, vmem_limit_bytes=VMEM_LIMIT
        ),
        name="assemble_and_send",
    )(b_count, refined, b_rows, b_coef, jnp.transpose(modes, (1, 0, 2)), owner, factor_inv)
    blocks, turned = pl.pallas_call(
        functools.partial(put_in_order, slots, slots * mode_count),
        out_shape=(
            jax.ShapeDtypeStruct((refined.shape[1], share, width), BF16),
            jax.ShapeDtypeStruct((lam_dev, groups * parts * slots * mode_count), F32),
        ),
        in_specs=[smem, vmem, vmem],
        out_specs=(vmem, vmem),
        compiler_params=pltpu.CompilerParams(vmem_limit_bytes=16 * 1024 * 1024),
        name="put_in_order",
    )(refined, dual, coarse)
    return blocks, turned.T


def solution(mesh):
    groups, parts = mesh.shape["row"], mesh.shape["help"]
    lam_dev = 16
    in_specs = (
        P(("row", "help"), None, None),
        P(("row", "help"), None),
        P(("row", "help"), None),
        P(("row", "help")),
        P("row", None),
        P(("row", "help"), None, None),
        P(("row", "help"), None),
    )
    out_specs = (P("row", "help", None), P(None, "row"))

    def body(*args):
        return on_device(groups, parts, *args, lam_dev)

    return jax.shard_map(body, mesh=mesh, in_specs=in_specs, out_specs=out_specs, check_vma=False)
```

```python
import functools

import jax
import jax.numpy as jnp
from jax import lax
from jax.experimental import pallas as pl
from jax.experimental.pallas import tpu as pltpu
from jax.sharding import PartitionSpec as P

MESH = pl.DeviceIdType.MESH
BF16 = jnp.bfloat16
F32 = jnp.float32
SLOT_ROWS = 8
LANES = 128
X_TILE = 256
GRAM_TILE = 256
VMEM_LIMIT = 28 * 1024 * 1024
ROW_X = 4


def one_hot(rows, count):
    at = lax.broadcasted_iota(jnp.int32, (count, rows.shape[1]), 0)
    return jnp.where(at == rows, F32(1.0), F32(0.0)).astype(BF16)


def two_parts(x):
    high = x.astype(BF16)
    low = (x - high.astype(F32)).astype(BF16)
    return jnp.concatenate([high, low], axis=0)


def sum_parts(x):
    half = x.shape[0] // 2
    return x[:half] + x[half:]


def ring_distance(step, size):
    return min(step, size - step)


def far_first(steps, sizes):
    def way(step):
        return -sum(ring_distance(a, n) for a, n in zip(step, sizes))
    return sorted((step for step in steps if any(step)), key=way)


def pick_lanes(table, rows):
    height, order = table.shape
    pieces = []
    for piece in range(rows.shape[1] // LANES):
        index = jnp.broadcast_to(rows[:, piece * LANES : (piece + 1) * LANES], (height, LANES))
        block, lane = lax.shift_right_logical(index, 7), lax.bitwise_and(index, LANES - 1)
        found = jnp.zeros((height, LANES), table.dtype)
        for source in range(order // LANES):
            values = jnp.take_along_axis(
                table[:, source * LANES : (source + 1) * LANES], lane, axis=1, mode="promise_in_bounds"
            )
            found = jnp.where(block == source, values, found)
        pieces.append(found)
    return jnp.concatenate(pieces, axis=1)


def assemble_and_send(
    groups, parts, lam_dev,
    count_hbm, refined_hbm, rows_hbm, coef_hbm, modes_hbm, owner_hbm, factor_hbm,
    blocks_ref, ordered_ref,
    count_ref, refined_ref, rows_ref, coef_ref, modes_ref, owner_ref,
    factor, picker, weight, stacked, panel, gram, term, terms, turned, coarse_ref, dual_ref,
    small_sem, load_sem, send_dual, recv_dual, send_term, recv_term, send_turn, recv_turn, send_pair, recv_pair, row_ready,
):
    row = lax.axis_index("row")
    part = lax.axis_index("help")
    core = part % 2
    chip = part // 2
    chips = parts // 2
    slots, order, _ = factor_hbm.shape
    width = rows_ref.shape[1]
    modes = modes_ref.shape[0]
    lam = groups * lam_dev
    share = width // parts

    small = [
        pltpu.make_async_copy(source, target, small_sem.at[number])
        for number, (source, target) in enumerate((
            (rows_hbm, rows_ref), (owner_hbm, owner_ref), (modes_hbm, modes_ref), (coef_hbm, coef_ref),
            (count_hbm, count_ref), (refined_hbm, refined_ref),
        ))
    ]
    for copy in small:
        copy.start()
    loads = []
    for tile in range(order // X_TILE):
        at = pl.ds(tile * X_TILE, X_TILE)
        loads.append(pltpu.make_async_copy(factor_hbm.at[:, at, :], factor[tile], load_sem.at[tile]))
        loads[-1].start()

    barrier = pltpu.get_barrier_semaphore()

    def greet_help(step, _):
        pl.semaphore_signal(barrier, inc=1, device_id=(row, (part + step) % parts), device_id_type=MESH)
        return 0

    head = groups // 2

    @pl.when(row != head)
    def _():
        pl.semaphore_signal(barrier, inc=1, device_id=(head, part), device_id_type=MESH)

    lax.fori_loop(1, parts, greet_help, 0)

    stacked[...] = jnp.zeros_like(stacked)
    column = lax.broadcasted_iota(jnp.int32, (1, width), 1)
    for copy in small:
        copy.wait()
    for slot in range(slots):
        stacked[slot * SLOT_ROWS : slot * SLOT_ROWS + modes, :] = modes_ref[:, slot, :]
        weight[slot] = jnp.where(column < count_ref[slot], coef_ref[slot : slot + 1, :], F32(0.0))
    totals = []
    for slot in range(slots):
        table = stacked[slot * SLOT_ROWS : (slot + 1) * SLOT_ROWS, :]
        values = pick_lanes(table, rows_ref[slot : slot + 1, :]) * weight[slot]
        owned = one_hot(owner_ref[slot : slot + 1, :], lam)
        totals.append(sum_parts(
            lax.dot_general(two_parts(values), owned, (((1,), (1,)), ((), ())), preferred_element_type=F32)
        ))
    total = jnp.concatenate(totals, axis=0).astype(BF16)
    term[...] = total
    terms[chip] = total

    def start(copy):
        def body(step, _):
            copy(step).start()
            return 0
        return body

    def arrived(copy):
        def body(step, _):
            copy(step).wait_recv()
            return 0
        return body

    def sent(copy):
        def body(step, _):
            copy(step).wait_send()
            return 0
        return body

    def term_copy(step):
        other = (chip + step) % chips
        return pltpu.make_async_remote_copy(
            src_ref=term, dst_ref=terms.at[chip],
            send_sem=send_term.at[step], recv_sem=recv_term.at[step],
            device_id=(row, other * 2 + core), device_id_type=MESH,
        )

    def term_arrival(step):
        other = (chip + chips - step) % chips
        return pltpu.make_async_remote_copy(
            src_ref=term, dst_ref=terms.at[other],
            send_sem=send_term.at[step], recv_sem=recv_term.at[step],
            device_id=(row, other * 2 + core), device_id_type=MESH,
        )

    def row_is_here(step, _):
        pl.semaphore_signal(row_ready, inc=1, device_id=((row + step) % groups, part), device_id_type=MESH)
        return 0

    def meet_and_send_terms():
        pl.semaphore_wait(barrier, parts - 1 + jnp.where(row == head, groups - 1, 0))

        @pl.when(row == head)
        def _():
            lax.fori_loop(1, groups, row_is_here, 0)

        for (step,) in far_first([(z,) for z in range(chips)], (chips,)):
            term_copy(step).start()

    late = chip >= chips // 2

    @pl.when(late)
    def _():
        meet_and_send_terms()

    chosen = jnp.int32(0)
    for entry in range(refined_ref.shape[1]):
        listed = refined_ref[0, entry]
        chosen = jnp.where(listed == part * slots + 1, jnp.int32(1), chosen)
    rows_here = jnp.where(chosen == 1, rows_ref[1:2, :], rows_ref[0:1, :])
    picker[...] = one_hot(rows_here, order)
    scale = weight[chosen]
    for tile in range(order // X_TILE):
        loads[tile].wait()
        picked = jnp.dot(factor[tile][chosen], picker[...], preferred_element_type=F32)
        panel[pl.ds(tile * X_TILE, X_TILE), :] = (picked * scale).astype(BF16)
    for tile in range(width // GRAM_TILE):
        at = pl.ds(tile * GRAM_TILE, GRAM_TILE)
        gram[at, :] = lax.dot_general(
            panel[:, at], panel[...], (((0,), (0,)), ((), ())), preferred_element_type=F32
        ).astype(BF16)

    def dual_copy(step):
        other = (chip + step // 2) % chips * 2 + (core + step % 2) % 2
        return pltpu.make_async_remote_copy(
            src_ref=gram.at[pl.ds(other * share, share), :], dst_ref=dual_ref.at[part],
            send_sem=send_dual.at[step], recv_sem=recv_dual.at[step],
            device_id=(row, other), device_id_type=MESH,
        )

    def dual_arrival(step):
        other = (chip + chips - step // 2) % chips * 2 + (core + step % 2) % 2
        return pltpu.make_async_remote_copy(
            src_ref=gram.at[pl.ds(other * share, share), :], dst_ref=dual_ref.at[other],
            send_sem=send_dual.at[step], recv_sem=recv_dual.at[step],
            device_id=(row, other), device_id_type=MESH,
        )

    @pl.when(jnp.logical_not(late))
    def _():
        meet_and_send_terms()

    for z, other_core in far_first([(z, c) for z in range(chips) for c in range(2)], (chips, 2)):
        dual_copy(2 * z + other_core).start()
    dual_ref[part] = gram[pl.ds(part * share, share), :]

    lax.fori_loop(1, chips, arrived(term_arrival), 0)
    lanes = chips * slots * SLOT_ROWS
    beside = terms[...].reshape(lanes, lam)
    turned[...] = jnp.transpose(beside.astype(F32)).astype(BF16)

    y, x = row // ROW_X, row % ROW_X
    row_y = groups // ROW_X

    def turn_copy(step):
        other = (y + step // ROW_X) % row_y * ROW_X + (x + step % ROW_X) % ROW_X
        return pltpu.make_async_remote_copy(
            src_ref=turned.at[pl.ds(other * lam_dev, lam_dev), :], dst_ref=coarse_ref.at[core, row],
            send_sem=send_turn.at[step], recv_sem=recv_turn.at[step],
            device_id=(other, part), device_id_type=MESH,
        )

    def turn_arrival(step):
        other = (y + row_y - step // ROW_X) % row_y * ROW_X + (x + ROW_X - step % ROW_X) % ROW_X
        return pltpu.make_async_remote_copy(
            src_ref=turned.at[pl.ds(other * lam_dev, lam_dev), :], dst_ref=coarse_ref.at[core, other],
            send_sem=send_turn.at[step], recv_sem=recv_turn.at[step],
            device_id=(other, part), device_id_type=MESH,
        )

    @pl.when(row != head)
    def _():
        pl.semaphore_wait(row_ready, 1)

    for step_y, step_x in far_first([(a, b) for a in range(row_y) for b in range(ROW_X)], (row_y, ROW_X)):
        turn_copy(ROW_X * step_y + step_x).start()
    coarse_ref[core, row] = turned[pl.ds(row * lam_dev, lam_dev), :]

    source = lax.broadcasted_iota(jnp.int32, (2 * lanes, 1), 0)
    from_core, inside = source // lanes, source % lanes
    from_chip, at = inside // (slots * SLOT_ROWS), inside % (slots * SLOT_ROWS)
    from_slot, mode = at // SLOT_ROWS, at % SLOT_ROWS
    target = jnp.where(mode < modes, ((from_chip * 2 + from_core) * slots + from_slot) * modes + mode, -512)
    lane = lax.broadcasted_iota(jnp.int32, (2 * lanes, 2 * lanes), 1)
    shift = parts * slots * modes - lanes
    to_even = jnp.where(lane == target, F32(1.0), F32(0.0)).astype(BF16)
    to_odd = jnp.where(lane == target + shift, F32(1.0), F32(0.0)).astype(BF16)

    lax.fori_loop(1, groups, arrived(turn_arrival), 0)

    there = chip * 2 + 1 - core
    pair_copy = pltpu.make_async_remote_copy(
        src_ref=coarse_ref.at[core], dst_ref=coarse_ref.at[core],
        send_sem=send_pair, recv_sem=recv_pair,
        device_id=(row, there), device_id_type=MESH,
    )
    pair_arrival = pltpu.make_async_remote_copy(
        src_ref=coarse_ref.at[1 - core], dst_ref=coarse_ref.at[1 - core],
        send_sem=send_pair, recv_sem=recv_pair,
        device_id=(row, there), device_id_type=MESH,
    )
    pair_copy.start()
    pair_arrival.wait_recv()
    halves = jnp.concatenate([coarse_ref[c].reshape(groups * lam_dev, lanes) for c in range(2)], axis=1)
    even = jnp.dot(halves, to_even, preferred_element_type=F32)
    odd = jnp.dot(halves, to_odd, preferred_element_type=F32)
    for pair in range(groups // 2):
        first = even[2 * pair * lam_dev : (2 * pair + 1) * lam_dev]
        second = odd[(2 * pair + 1) * lam_dev : (2 * pair + 2) * lam_dev]
        base = pair * 3 * lanes
        ordered_ref[:, base : base + lanes] = first[:, :lanes]
        ordered_ref[:, base + lanes : base + 2 * lanes] = first[:, lanes:] + second[:, :lanes]
        ordered_ref[:, base + 2 * lanes : base + 3 * lanes] = second[:, lanes:]

    pair_copy.wait_send()
    lax.fori_loop(1, chips, sent(term_copy), 0)
    lax.fori_loop(1, groups, sent(turn_copy), 0)
    lax.fori_loop(1, parts, sent(dual_copy), 0)
    lax.fori_loop(1, parts, arrived(dual_arrival), 0)
    for entry in range(refined_ref.shape[1]):
        blocks_ref[entry] = dual_ref[lax.shift_right_logical(refined_ref[0, entry], slots - 1)]


def on_device(groups, parts, factor_inv, b_rows, b_coef, b_count, refined, modes, owner, lam_dev):
    slots, order, _ = factor_inv.shape
    width = b_rows.shape[1]
    mode_count = modes.shape[1]
    share = width // parts
    chips = parts // 2
    rows = slots * SLOT_ROWS
    lanes = chips * rows
    lam = groups * lam_dev
    columns = groups * parts * slots * mode_count
    vmem = pl.BlockSpec(memory_space=pltpu.VMEM)
    anywhere = pl.BlockSpec(memory_space=pl.ANY)
    inputs = (b_count, refined, b_rows, b_coef, jnp.transpose(modes, (1, 0, 2)), owner, factor_inv)
    blocks, ordered = pl.pallas_call(
        functools.partial(assemble_and_send, groups, parts, lam_dev),
        out_shape=(
            pltpu.VMEM((refined.shape[1], share, width), BF16),
            pltpu.VMEM((lam_dev, columns), F32),
        ),
        in_specs=[anywhere] * 7,
        out_specs=(vmem, vmem),
        scratch_shapes=[
            pltpu.SMEM(b_count.shape, jnp.int32),
            pltpu.SMEM(refined.shape, jnp.int32),
            pltpu.VMEM(b_rows.shape, jnp.int32),
            pltpu.VMEM(b_coef.shape, F32),
            pltpu.VMEM((mode_count, slots, order), F32),
            pltpu.VMEM(owner.shape, jnp.int32),
            [pltpu.VMEM((slots, X_TILE, order), BF16) for _ in range(order // X_TILE)],
            pltpu.VMEM((order, width), BF16),
            pltpu.VMEM((slots, 1, width), F32),
            pltpu.VMEM((rows, order), F32),
            pltpu.VMEM((order, width), BF16),
            pltpu.VMEM((width, width), BF16),
            pltpu.VMEM((rows, lam), BF16),
            pltpu.VMEM((chips, rows, lam), BF16),
            pltpu.VMEM((lam, lanes), BF16),
            pltpu.VMEM((2, groups, lam_dev, lanes), BF16),
            pltpu.VMEM((parts, share, width), BF16),
            pltpu.SemaphoreType.DMA((6,)),
            pltpu.SemaphoreType.DMA((order // X_TILE,)),
            pltpu.SemaphoreType.DMA((parts,)),
            pltpu.SemaphoreType.DMA((parts,)),
            pltpu.SemaphoreType.DMA((chips,)),
            pltpu.SemaphoreType.DMA((chips,)),
            pltpu.SemaphoreType.DMA((groups,)),
            pltpu.SemaphoreType.DMA((groups,)),
            pltpu.SemaphoreType.DMA,
            pltpu.SemaphoreType.DMA,
            pltpu.SemaphoreType.REGULAR,
        ],
        compiler_params=pltpu.CompilerParams(
            collective_id=0, has_side_effects=True, vmem_limit_bytes=VMEM_LIMIT
        ),
        name="assemble_and_send",
    )(*(pltpu.with_memory_space_constraint(array, pltpu.HBM) for array in inputs))
    return blocks, ordered.T


def solution(mesh):
    groups, parts = mesh.shape["row"], mesh.shape["help"]
    lam_dev = 16
    in_specs = (
        P(("row", "help"), None, None),
        P(("row", "help"), None),
        P(("row", "help"), None),
        P(("row", "help")),
        P("row", None),
        P(("row", "help"), None, None),
        P(("row", "help"), None),
    )
    out_specs = (P("row", "help", None), P(None, "row"))

    def body(*args):
        return on_device(groups, parts, *args, lam_dev)

    return jax.shard_map(body, mesh=mesh, in_specs=in_specs, out_specs=out_specs, check_vma=False)
```

```python
import functools

import jax
import jax.numpy as jnp
from jax import lax
from jax.experimental import pallas as pl
from jax.experimental.pallas import tpu as pltpu
from jax.sharding import PartitionSpec as P

MESH = pl.DeviceIdType.MESH
BF16 = jnp.bfloat16
F32 = jnp.float32
SLOT_ROWS = 8
LANES = 128
X_TILE = 256
GRAM_TILE = 256
VMEM_LIMIT = 28 * 1024 * 1024
ROW_X = 4


def one_hot(rows, count):
    at = lax.broadcasted_iota(jnp.int32, (count, rows.shape[1]), 0)
    return jnp.where(at == rows, F32(1.0), F32(0.0)).astype(BF16)


def two_parts(x):
    high = x.astype(BF16)
    low = (x - high.astype(F32)).astype(BF16)
    return jnp.concatenate([high, low], axis=0)


def sum_parts(x):
    half = x.shape[0] // 2
    return x[:half] + x[half:]


def ring_distance(step, size):
    return min(step, size - step)


def far_first(steps, sizes):
    def way(step):
        return -sum(ring_distance(a, n) for a, n in zip(step, sizes))
    return sorted((step for step in steps if any(step)), key=way)


def owner_place(owner, x, lam_dev, column_share):
    shift = lam_dev.bit_length() - 1
    holder = lax.shift_right_logical(owner, shift)
    place = lax.bitwise_and(x + 2 - lax.bitwise_and(holder, ROW_X - 1), ROW_X - 1)
    holder_y = lax.shift_right_logical(holder, ROW_X.bit_length() - 1)
    return place * column_share + holder_y * lam_dev + lax.bitwise_and(owner, lam_dev - 1)


def pick_lanes(table, rows):
    height, order = table.shape
    pieces = []
    for piece in range(rows.shape[1] // LANES):
        index = jnp.broadcast_to(rows[:, piece * LANES : (piece + 1) * LANES], (height, LANES))
        block, lane = lax.shift_right_logical(index, 7), lax.bitwise_and(index, LANES - 1)
        found = jnp.zeros((height, LANES), table.dtype)
        for source in range(order // LANES):
            values = jnp.take_along_axis(
                table[:, source * LANES : (source + 1) * LANES], lane, axis=1, mode="promise_in_bounds"
            )
            found = jnp.where(block == source, values, found)
        pieces.append(found)
    return jnp.concatenate(pieces, axis=1)


def assemble_and_send(
    groups, parts, lam_dev,
    count_hbm, refined_hbm, rows_hbm, coef_hbm, modes_hbm, owner_hbm, factor_hbm,
    blocks_ref, ordered_ref,
    count_ref, refined_ref, rows_ref, coef_ref, modes_ref, owner_ref,
    factor, picker, weight, stacked, panel, gram, term, terms, turned, coarse_ref, dual_ref,
    small_sem, load_sem, send_dual, recv_dual, send_term, recv_term, send_turn, recv_turn, send_pair, recv_pair, row_ready,
):
    row = lax.axis_index("row")
    part = lax.axis_index("help")
    core = part % 2
    chip = part // 2
    chips = parts // 2
    slots, order, _ = factor_hbm.shape
    width = rows_ref.shape[1]
    modes = modes_ref.shape[0]
    lam = groups * lam_dev
    share = width // parts
    y, x = row // ROW_X, row % ROW_X
    row_y = groups // ROW_X
    column_share = row_y * lam_dev
    half_width = lam // 2

    small = [
        pltpu.make_async_copy(source, target, small_sem.at[number])
        for number, (source, target) in enumerate((
            (rows_hbm, rows_ref), (owner_hbm, owner_ref), (modes_hbm, modes_ref), (coef_hbm, coef_ref),
            (count_hbm, count_ref), (refined_hbm, refined_ref),
        ))
    ]
    for copy in small:
        copy.start()
    loads = []
    for tile in range(order // X_TILE):
        at = pl.ds(tile * X_TILE, X_TILE)
        loads.append(pltpu.make_async_copy(factor_hbm.at[:, at, :], factor[tile], load_sem.at[tile]))
        loads[-1].start()

    barrier = pltpu.get_barrier_semaphore()

    def greet_help(step, _):
        pl.semaphore_signal(barrier, inc=1, device_id=(row, (part + step) % parts), device_id_type=MESH)
        return 0

    head = groups // 2

    @pl.when(row != head)
    def _():
        pl.semaphore_signal(barrier, inc=1, device_id=(head, part), device_id_type=MESH)

    lax.fori_loop(1, parts, greet_help, 0)

    stacked[...] = jnp.zeros_like(stacked)
    column = lax.broadcasted_iota(jnp.int32, (1, width), 1)
    for copy in small:
        copy.wait()
    for slot in range(slots):
        stacked[slot * SLOT_ROWS : slot * SLOT_ROWS + modes, :] = modes_ref[:, slot, :]
        weight[slot] = jnp.where(column < count_ref[slot], coef_ref[slot : slot + 1, :], F32(0.0))
    totals = []
    for slot in range(slots):
        table = stacked[slot * SLOT_ROWS : (slot + 1) * SLOT_ROWS, :]
        values = pick_lanes(table, rows_ref[slot : slot + 1, :]) * weight[slot]
        owned = one_hot(owner_place(owner_ref[slot : slot + 1, :], x, lam_dev, column_share), lam)
        totals.append(sum_parts(
            lax.dot_general(two_parts(values), owned, (((1,), (1,)), ((), ())), preferred_element_type=F32)
        ))
    total = jnp.concatenate(totals, axis=0).astype(BF16)
    term[...] = total
    terms[chip] = total

    def start(copy):
        def body(step, _):
            copy(step).start()
            return 0
        return body

    def arrived(copy):
        def body(step, _):
            copy(step).wait_recv()
            return 0
        return body

    def sent(copy):
        def body(step, _):
            copy(step).wait_send()
            return 0
        return body

    def term_copy(step):
        other = (chip + step % chips) % chips
        at = pl.ds(pl.multiple_of(step // chips * half_width, half_width), half_width)
        return pltpu.make_async_remote_copy(
            src_ref=term.at[:, at], dst_ref=terms.at[chip, :, at],
            send_sem=send_term.at[step], recv_sem=recv_term.at[step],
            device_id=(row, other * 2 + core), device_id_type=MESH,
        )

    def term_arrival(step):
        other = (chip + chips - step % chips) % chips
        at = pl.ds(pl.multiple_of(step // chips * half_width, half_width), half_width)
        return pltpu.make_async_remote_copy(
            src_ref=term.at[:, at], dst_ref=terms.at[other, :, at],
            send_sem=send_term.at[step], recv_sem=recv_term.at[step],
            device_id=(row, other * 2 + core), device_id_type=MESH,
        )

    def row_is_here(step, _):
        pl.semaphore_signal(row_ready, inc=1, device_id=((row + step) % groups, part), device_id_type=MESH)
        return 0

    def meet_and_send_terms():
        pl.semaphore_wait(barrier, parts - 1 + jnp.where(row == head, groups - 1, 0))

        @pl.when(row == head)
        def _():
            lax.fori_loop(1, groups, row_is_here, 0)

        for half in range(2):
            for (step,) in far_first([(z,) for z in range(chips)], (chips,)):
                term_copy(half * chips + step).start()

    late = chip >= chips // 2

    @pl.when(late)
    def _():
        meet_and_send_terms()

    chosen = jnp.int32(0)
    for entry in range(refined_ref.shape[1]):
        listed = refined_ref[0, entry]
        chosen = jnp.where(listed == part * slots + 1, jnp.int32(1), chosen)
    rows_here = jnp.where(chosen == 1, rows_ref[1:2, :], rows_ref[0:1, :])
    picker[...] = one_hot(rows_here, order)
    scale = weight[chosen]
    for tile in range(order // X_TILE):
        loads[tile].wait()
        picked = jnp.dot(factor[tile][chosen], picker[...], preferred_element_type=F32)
        panel[pl.ds(tile * X_TILE, X_TILE), :] = (picked * scale).astype(BF16)
    for tile in range(width // GRAM_TILE):
        at = pl.ds(tile * GRAM_TILE, GRAM_TILE)
        gram[at, :] = lax.dot_general(
            panel[:, at], panel[...], (((0,), (0,)), ((), ())), preferred_element_type=F32
        ).astype(BF16)

    def dual_copy(step):
        other = (chip + step // 2) % chips * 2 + (core + step % 2) % 2
        return pltpu.make_async_remote_copy(
            src_ref=gram.at[pl.ds(other * share, share), :], dst_ref=dual_ref.at[part],
            send_sem=send_dual.at[step], recv_sem=recv_dual.at[step],
            device_id=(row, other), device_id_type=MESH,
        )

    def dual_arrival(step):
        other = (chip + chips - step // 2) % chips * 2 + (core + step % 2) % 2
        return pltpu.make_async_remote_copy(
            src_ref=gram.at[pl.ds(other * share, share), :], dst_ref=dual_ref.at[other],
            send_sem=send_dual.at[step], recv_sem=recv_dual.at[step],
            device_id=(row, other), device_id_type=MESH,
        )

    @pl.when(jnp.logical_not(late))
    def _():
        meet_and_send_terms()

    for z, other_core in far_first([(z, c) for z in range(chips) for c in range(2)], (chips, 2)):
        dual_copy(2 * z + other_core).start()
    dual_ref[part] = gram[pl.ds(part * share, share), :]

    lanes = chips * slots * SLOT_ROWS

    def turn_copy(step):
        other_y, other_x = (y + step // ROW_X) % row_y, (x + step % ROW_X) % ROW_X
        start_row = (ROW_X + 2 - step % ROW_X) % ROW_X * column_share + other_y * lam_dev
        return pltpu.make_async_remote_copy(
            src_ref=turned.at[pl.ds(pl.multiple_of(start_row, lam_dev), lam_dev), :],
            dst_ref=coarse_ref.at[core, x * row_y + y],
            send_sem=send_turn.at[step], recv_sem=recv_turn.at[step],
            device_id=(other_y * ROW_X + other_x, part), device_id_type=MESH,
        )

    def turn_arrival(step):
        other_y, other_x = (y + row_y - step // ROW_X) % row_y, (x + ROW_X - step % ROW_X) % ROW_X
        return pltpu.make_async_remote_copy(
            src_ref=turned.at[pl.ds(0, lam_dev), :], dst_ref=coarse_ref.at[core, other_x * row_y + other_y],
            send_sem=send_turn.at[step], recv_sem=recv_turn.at[step],
            device_id=(other_y * ROW_X + other_x, part), device_id_type=MESH,
        )

    @pl.when(row != head)
    def _():
        pl.semaphore_wait(row_ready, 1)

    halves_of_x = ((2, 1), (0, 3))
    for half, steps_x in enumerate(halves_of_x):
        lax.fori_loop(half * chips + 1, (half + 1) * chips, arrived(term_arrival), 0)
        at = slice(half * half_width, (half + 1) * half_width)
        beside = terms[:, :, at].reshape(lanes, half_width)
        turned[at, :] = jnp.transpose(beside.astype(F32)).astype(BF16)
        for step_y, step_x in far_first([(a, b) for a in range(row_y) for b in steps_x], (row_y, ROW_X)):
            turn_copy(ROW_X * step_y + step_x).start()
    coarse_ref[core, x * row_y + y] = turned[pl.ds(2 * column_share + y * lam_dev, lam_dev), :]

    source = lax.broadcasted_iota(jnp.int32, (2 * lanes, 1), 0)
    from_core, inside = source // lanes, source % lanes
    from_chip, at = inside // (slots * SLOT_ROWS), inside % (slots * SLOT_ROWS)
    from_slot, mode = at // SLOT_ROWS, at % SLOT_ROWS
    target = jnp.where(mode < modes, ((from_chip * 2 + from_core) * slots + from_slot) * modes + mode, -512)
    lane = lax.broadcasted_iota(jnp.int32, (2 * lanes, 2 * lanes), 1)
    shift = parts * slots * modes - lanes
    to_even = jnp.where(lane == target, F32(1.0), F32(0.0)).astype(BF16)
    to_odd = jnp.where(lane == target + shift, F32(1.0), F32(0.0)).astype(BF16)

    there = chip * 2 + 1 - core

    def pair_copy(step_x, half):
        at = pl.ds((x + ROW_X - step_x) % ROW_X * row_y, row_y)
        return pltpu.make_async_remote_copy(
            src_ref=coarse_ref.at[half, at], dst_ref=coarse_ref.at[half, at],
            send_sem=send_pair.at[step_x], recv_sem=recv_pair.at[step_x],
            device_id=(row, there), device_id_type=MESH,
        )

    for steps_x in halves_of_x:
        for step_x in steps_x:
            for step_y in range(row_y):
                if step_y or step_x:
                    turn_arrival(ROW_X * step_y + step_x).wait_recv()
            pair_copy(step_x, core).start()
    for step_x in range(ROW_X):
        pair_copy(step_x, 1 - core).wait_recv()
    halves = jnp.concatenate([coarse_ref[c].reshape(groups * lam_dev, lanes) for c in range(2)], axis=1)
    even = jnp.dot(halves, to_even, preferred_element_type=F32)
    odd = jnp.dot(halves, to_odd, preferred_element_type=F32)
    for pair in range(groups // 2):
        kept = [(number % ROW_X * row_y + number // ROW_X) * lam_dev for number in (2 * pair, 2 * pair + 1)]
        first = even[kept[0] : kept[0] + lam_dev]
        second = odd[kept[1] : kept[1] + lam_dev]
        base = pair * 3 * lanes
        ordered_ref[:, base : base + lanes] = first[:, :lanes]
        ordered_ref[:, base + lanes : base + 2 * lanes] = first[:, lanes:] + second[:, :lanes]
        ordered_ref[:, base + 2 * lanes : base + 3 * lanes] = second[:, lanes:]

    for step_x in range(ROW_X):
        pair_copy(step_x, core).wait_send()
    for half in range(2):
        lax.fori_loop(half * chips + 1, (half + 1) * chips, sent(term_copy), 0)
    lax.fori_loop(1, groups, sent(turn_copy), 0)
    lax.fori_loop(1, parts, sent(dual_copy), 0)
    lax.fori_loop(1, parts, arrived(dual_arrival), 0)
    for entry in range(refined_ref.shape[1]):
        blocks_ref[entry] = dual_ref[lax.shift_right_logical(refined_ref[0, entry], slots - 1)]


def write_out(blocks_ref, ordered_ref, blocks_out, ordered_out, sem):
    copies = []
    for number, (source, target) in enumerate(((blocks_ref, blocks_out), (ordered_ref, ordered_out))):
        half = source.shape[0] // 2
        for at in range(2):
            rows = pl.ds(at * half, half)
            copies.append(pltpu.make_async_copy(source.at[rows], target.at[rows], sem.at[2 * number + at]))
    for copy in copies:
        copy.start()
    for copy in copies:
        copy.wait()


def on_device(groups, parts, factor_inv, b_rows, b_coef, b_count, refined, modes, owner, lam_dev):
    slots, order, _ = factor_inv.shape
    width = b_rows.shape[1]
    mode_count = modes.shape[1]
    share = width // parts
    chips = parts // 2
    rows = slots * SLOT_ROWS
    lanes = chips * rows
    lam = groups * lam_dev
    columns = groups * parts * slots * mode_count
    vmem = pl.BlockSpec(memory_space=pltpu.VMEM)
    anywhere = pl.BlockSpec(memory_space=pl.ANY)
    inputs = (b_count, refined, b_rows, b_coef, jnp.transpose(modes, (1, 0, 2)), owner, factor_inv)
    blocks, ordered = pl.pallas_call(
        functools.partial(assemble_and_send, groups, parts, lam_dev),
        out_shape=(
            pltpu.VMEM((refined.shape[1], share, width), BF16),
            pltpu.VMEM((lam_dev, columns), F32),
        ),
        in_specs=[anywhere] * 7,
        out_specs=(vmem, vmem),
        scratch_shapes=[
            pltpu.SMEM(b_count.shape, jnp.int32),
            pltpu.SMEM(refined.shape, jnp.int32),
            pltpu.VMEM(b_rows.shape, jnp.int32),
            pltpu.VMEM(b_coef.shape, F32),
            pltpu.VMEM((mode_count, slots, order), F32),
            pltpu.VMEM(owner.shape, jnp.int32),
            [pltpu.VMEM((slots, X_TILE, order), BF16) for _ in range(order // X_TILE)],
            pltpu.VMEM((order, width), BF16),
            pltpu.VMEM((slots, 1, width), F32),
            pltpu.VMEM((rows, order), F32),
            pltpu.VMEM((order, width), BF16),
            pltpu.VMEM((width, width), BF16),
            pltpu.VMEM((rows, lam), BF16),
            pltpu.VMEM((chips, rows, lam), BF16),
            pltpu.VMEM((lam, lanes), BF16),
            pltpu.VMEM((2, groups, lam_dev, lanes), BF16),
            pltpu.VMEM((parts, share, width), BF16),
            pltpu.SemaphoreType.DMA((6,)),
            pltpu.SemaphoreType.DMA((order // X_TILE,)),
            pltpu.SemaphoreType.DMA((parts,)),
            pltpu.SemaphoreType.DMA((parts,)),
            pltpu.SemaphoreType.DMA((2 * chips,)),
            pltpu.SemaphoreType.DMA((2 * chips,)),
            pltpu.SemaphoreType.DMA((groups,)),
            pltpu.SemaphoreType.DMA((groups,)),
            pltpu.SemaphoreType.DMA((ROW_X,)),
            pltpu.SemaphoreType.DMA((ROW_X,)),
            pltpu.SemaphoreType.REGULAR,
        ],
        compiler_params=pltpu.CompilerParams(
            collective_id=0, has_side_effects=True, vmem_limit_bytes=VMEM_LIMIT
        ),
        name="assemble_and_send",
    )(*(pltpu.with_memory_space_constraint(array, pltpu.HBM) for array in inputs))
    blocks, ordered = pl.pallas_call(
        write_out,
        out_shape=(
            jax.ShapeDtypeStruct(blocks.shape, BF16),
            jax.ShapeDtypeStruct(ordered.shape, F32),
        ),
        in_specs=[vmem, vmem],
        out_specs=(anywhere, anywhere),
        scratch_shapes=[pltpu.SemaphoreType.DMA((4,))],
        compiler_params=pltpu.CompilerParams(vmem_limit_bytes=2 * 1024 * 1024),
        name="write_out",
    )(*(pltpu.with_memory_space_constraint(array, pltpu.VMEM) for array in (blocks, ordered)))
    return blocks, ordered.T


def solution(mesh):
    groups, parts = mesh.shape["row"], mesh.shape["help"]
    lam_dev = 16
    in_specs = (
        P(("row", "help"), None, None),
        P(("row", "help"), None),
        P(("row", "help"), None),
        P(("row", "help")),
        P("row", None),
        P(("row", "help"), None, None),
        P(("row", "help"), None),
    )
    out_specs = (P("row", "help", None), P(None, "row"))

    def body(*args):
        return on_device(groups, parts, *args, lam_dev)

    return jax.shard_map(body, mesh=mesh, in_specs=in_specs, out_specs=out_specs, check_vma=False)
```

```python
import functools

import jax
import jax.numpy as jnp
from jax import lax
from jax.experimental import pallas as pl
from jax.experimental.pallas import tpu as pltpu
from jax.sharding import PartitionSpec as P

MESH = pl.DeviceIdType.MESH
BF16 = jnp.bfloat16
F32 = jnp.float32
SLOT_ROWS = 8
LANES = 128
X_TILE = 256
GRAM_TILE = 256
VMEM_LIMIT = 28 * 1024 * 1024
ROW_X = 4


def one_hot(rows, count):
    at = lax.broadcasted_iota(jnp.int32, (count, rows.shape[1]), 0)
    return jnp.where(at == rows, F32(1.0), F32(0.0)).astype(BF16)


def two_parts(x):
    high = x.astype(BF16)
    low = (x - high.astype(F32)).astype(BF16)
    return jnp.concatenate([high, low], axis=0)


def sum_parts(x):
    half = x.shape[0] // 2
    return x[:half] + x[half:]


def ring_distance(step, size):
    return min(step, size - step)


def far_first(steps, sizes):
    def way(step):
        return -sum(ring_distance(a, n) for a, n in zip(step, sizes))
    return sorted((step for step in steps if any(step)), key=way)


def owner_place(owner, x, lam_dev, column_share):
    shift = lam_dev.bit_length() - 1
    holder = lax.shift_right_logical(owner, shift)
    place = lax.bitwise_and(x + 2 - lax.bitwise_and(holder, ROW_X - 1), ROW_X - 1)
    holder_y = lax.shift_right_logical(holder, ROW_X.bit_length() - 1)
    return place * column_share + holder_y * lam_dev + lax.bitwise_and(owner, lam_dev - 1)


def pick_lanes(table, rows):
    height, order = table.shape
    pieces = []
    for piece in range(rows.shape[1] // LANES):
        index = jnp.broadcast_to(rows[:, piece * LANES : (piece + 1) * LANES], (height, LANES))
        block, lane = lax.shift_right_logical(index, 7), lax.bitwise_and(index, LANES - 1)
        found = jnp.zeros((height, LANES), table.dtype)
        for source in range(order // LANES):
            values = jnp.take_along_axis(
                table[:, source * LANES : (source + 1) * LANES], lane, axis=1, mode="promise_in_bounds"
            )
            found = jnp.where(block == source, values, found)
        pieces.append(found)
    return jnp.concatenate(pieces, axis=1)


def assemble_and_send(
    groups, parts, lam_dev,
    count_hbm, refined_hbm, rows_hbm, coef_hbm, modes_hbm, owner_hbm, factor_hbm,
    blocks_ref, ordered_ref,
    count_ref, refined_ref, rows_ref, coef_ref, modes_ref, owner_ref,
    factor, picker, weight, stacked, panel, gram, term, terms, turned, coarse_ref, dual_ref,
    small_sem, load_sem, send_dual, recv_dual, send_term, recv_term, send_turn, recv_turn, send_pair, recv_pair, row_ready,
):
    row = lax.axis_index("row")
    part = lax.axis_index("help")
    core = lax.rem(part, 2)
    chip = lax.div(part, 2)
    chips = parts // 2
    slots, order, _ = factor_hbm.shape
    width = rows_ref.shape[1]
    modes = modes_ref.shape[0]
    lam = groups * lam_dev
    share = width // parts
    y, x = lax.div(row, ROW_X), lax.rem(row, ROW_X)
    row_y = groups // ROW_X
    chip_ahead = [lax.rem(chip + step, chips) for step in range(chips)]
    chip_behind = [lax.rem(chip + chips - step, chips) for step in range(chips)]
    core_at = [core, 1 - core]
    y_ahead = [lax.rem(y + step, row_y) for step in range(row_y)]
    y_behind = [lax.rem(y + row_y - step, row_y) for step in range(row_y)]
    x_ahead = [lax.rem(x + step, ROW_X) for step in range(ROW_X)]
    x_behind = [lax.rem(x + ROW_X - step, ROW_X) for step in range(ROW_X)]
    column_share = row_y * lam_dev
    half_width = lam // 2

    small = [
        pltpu.make_async_copy(source, target, small_sem.at[number])
        for number, (source, target) in enumerate((
            (rows_hbm, rows_ref), (owner_hbm, owner_ref), (modes_hbm, modes_ref), (coef_hbm, coef_ref),
            (count_hbm, count_ref), (refined_hbm, refined_ref),
        ))
    ]
    for copy in small:
        copy.start()
    loads = []
    for tile in range(order // X_TILE):
        at = pl.ds(tile * X_TILE, X_TILE)
        loads.append(pltpu.make_async_copy(factor_hbm.at[:, at, :], factor[tile], load_sem.at[tile]))
        loads[-1].start()

    barrier = pltpu.get_barrier_semaphore()

    def greet_help(step, _):
        pl.semaphore_signal(barrier, inc=1, device_id=(row, lax.rem(part + step, parts)), device_id_type=MESH)
        return 0

    head = groups // 2

    @pl.when(row != head)
    def _():
        pl.semaphore_signal(barrier, inc=1, device_id=(head, part), device_id_type=MESH)

    lax.fori_loop(1, parts, greet_help, 0)

    stacked[...] = jnp.zeros_like(stacked)
    column = lax.broadcasted_iota(jnp.int32, (1, width), 1)
    for copy in small:
        copy.wait()
    for slot in range(slots):
        stacked[slot * SLOT_ROWS : slot * SLOT_ROWS + modes, :] = modes_ref[:, slot, :]
        weight[slot] = jnp.where(column < count_ref[slot], coef_ref[slot : slot + 1, :], F32(0.0))
    totals = []
    for slot in range(slots):
        table = stacked[slot * SLOT_ROWS : (slot + 1) * SLOT_ROWS, :]
        values = pick_lanes(table, rows_ref[slot : slot + 1, :]) * weight[slot]
        owned = one_hot(owner_place(owner_ref[slot : slot + 1, :], x, lam_dev, column_share), lam)
        totals.append(sum_parts(
            lax.dot_general(two_parts(values), owned, (((1,), (1,)), ((), ())), preferred_element_type=F32)
        ))
    total = jnp.concatenate(totals, axis=0).astype(BF16)
    term[...] = total
    terms[chip] = total

    def term_copy(step):
        other = chip_ahead[step % chips]
        at = pl.ds(step // chips * half_width, half_width)
        return pltpu.make_async_remote_copy(
            src_ref=term.at[:, at], dst_ref=terms.at[chip, :, at],
            send_sem=send_term.at[step], recv_sem=recv_term.at[step],
            device_id=(row, other * 2 + core), device_id_type=MESH,
        )

    def term_arrival(step):
        other = chip_behind[step % chips]
        at = pl.ds(step // chips * half_width, half_width)
        return pltpu.make_async_remote_copy(
            src_ref=term.at[:, at], dst_ref=terms.at[other, :, at],
            send_sem=send_term.at[step], recv_sem=recv_term.at[step],
            device_id=(row, other * 2 + core), device_id_type=MESH,
        )

    def row_is_here(step, _):
        pl.semaphore_signal(row_ready, inc=1, device_id=(lax.rem(row + step, groups), part), device_id_type=MESH)
        return 0

    def meet_and_send_terms():
        pl.semaphore_wait(barrier, parts - 1 + jnp.where(row == head, groups - 1, 0))

        @pl.when(row == head)
        def _():
            lax.fori_loop(1, groups, row_is_here, 0)

        for half in range(2):
            for (step,) in far_first([(z,) for z in range(chips)], (chips,)):
                term_copy(half * chips + step).start()

    late = chip >= chips // 2

    @pl.when(late)
    def _():
        meet_and_send_terms()

    chosen = jnp.int32(0)
    for entry in range(refined_ref.shape[1]):
        listed = refined_ref[0, entry]
        chosen = jnp.where(listed == part * slots + 1, jnp.int32(1), chosen)
    rows_here = jnp.where(chosen == 1, rows_ref[1:2, :], rows_ref[0:1, :])
    picker[...] = one_hot(rows_here, order)
    scale = weight[chosen]
    for tile in range(order // X_TILE):
        loads[tile].wait()
        picked = jnp.dot(factor[tile][chosen], picker[...], preferred_element_type=F32)
        panel[pl.ds(tile * X_TILE, X_TILE), :] = (picked * scale).astype(BF16)
    for tile in range(width // GRAM_TILE):
        at = pl.ds(tile * GRAM_TILE, GRAM_TILE)
        gram[at, :] = lax.dot_general(
            panel[:, at], panel[...], (((0,), (0,)), ((), ())), preferred_element_type=F32
        ).astype(BF16)

    def dual_copy(step):
        other = chip_ahead[step // 2] * 2 + core_at[step % 2]
        return pltpu.make_async_remote_copy(
            src_ref=gram.at[pl.ds(other * share, share), :], dst_ref=dual_ref.at[part],
            send_sem=send_dual.at[step], recv_sem=recv_dual.at[step],
            device_id=(row, other), device_id_type=MESH,
        )

    def dual_arrival(step):
        other = chip_behind[step // 2] * 2 + core_at[step % 2]
        return pltpu.make_async_remote_copy(
            src_ref=gram.at[pl.ds(other * share, share), :], dst_ref=dual_ref.at[other],
            send_sem=send_dual.at[step], recv_sem=recv_dual.at[step],
            device_id=(row, other), device_id_type=MESH,
        )

    @pl.when(jnp.logical_not(late))
    def _():
        meet_and_send_terms()

    for z, other_core in far_first([(z, c) for z in range(chips) for c in range(2)], (chips, 2)):
        dual_copy(2 * z + other_core).start()
    dual_ref[part] = gram[pl.ds(part * share, share), :]

    lanes = chips * slots * SLOT_ROWS

    def turn_copy(step):
        other_y, other_x = y_ahead[step // ROW_X], x_ahead[step % ROW_X]
        start_row = (ROW_X + 2 - step % ROW_X) % ROW_X * column_share + other_y * lam_dev
        return pltpu.make_async_remote_copy(
            src_ref=turned.at[pl.ds(pl.multiple_of(start_row, lam_dev), lam_dev), :],
            dst_ref=coarse_ref.at[core, x * row_y + y],
            send_sem=send_turn.at[step], recv_sem=recv_turn.at[step],
            device_id=(other_y * ROW_X + other_x, part), device_id_type=MESH,
        )

    def turn_arrival(step):
        other_y, other_x = y_behind[step // ROW_X], x_behind[step % ROW_X]
        return pltpu.make_async_remote_copy(
            src_ref=turned.at[pl.ds(0, lam_dev), :], dst_ref=coarse_ref.at[core, other_x * row_y + other_y],
            send_sem=send_turn.at[step], recv_sem=recv_turn.at[step],
            device_id=(other_y * ROW_X + other_x, part), device_id_type=MESH,
        )

    @pl.when(row != head)
    def _():
        pl.semaphore_wait(row_ready, 1)

    halves_of_x = ((2, 1), (0, 3))
    for half, steps_x in enumerate(halves_of_x):
        for step in range(1, chips):
            term_arrival(half * chips + step).wait_recv()
        at = slice(half * half_width, (half + 1) * half_width)
        beside = terms[:, :, at].reshape(lanes, half_width)
        turned[at, :] = jnp.transpose(beside.astype(F32)).astype(BF16)
        for step_y, step_x in far_first([(a, b) for a in range(row_y) for b in steps_x], (row_y, ROW_X)):
            turn_copy(ROW_X * step_y + step_x).start()
    coarse_ref[core, x * row_y + y] = turned[pl.ds(2 * column_share + y * lam_dev, lam_dev), :]

    source = lax.broadcasted_iota(jnp.int32, (2 * lanes, 1), 0)
    from_core, inside = source // lanes, source % lanes
    from_chip, at = inside // (slots * SLOT_ROWS), inside % (slots * SLOT_ROWS)
    from_slot, mode = at // SLOT_ROWS, at % SLOT_ROWS
    target = jnp.where(mode < modes, ((from_chip * 2 + from_core) * slots + from_slot) * modes + mode, -512)
    lane = lax.broadcasted_iota(jnp.int32, (2 * lanes, 2 * lanes), 1)
    shift = parts * slots * modes - lanes
    to_even = jnp.where(lane == target, F32(1.0), F32(0.0)).astype(BF16)
    to_odd = jnp.where(lane == target + shift, F32(1.0), F32(0.0)).astype(BF16)

    there = chip * 2 + 1 - core

    def pair_copy(step_x, half):
        at = pl.ds(x_behind[step_x] * row_y, row_y)
        return pltpu.make_async_remote_copy(
            src_ref=coarse_ref.at[half, at], dst_ref=coarse_ref.at[half, at],
            send_sem=send_pair.at[step_x], recv_sem=recv_pair.at[step_x],
            device_id=(row, there), device_id_type=MESH,
        )

    for steps_x in halves_of_x:
        for step_x in steps_x:
            for step_y in range(row_y):
                if step_y or step_x:
                    turn_arrival(ROW_X * step_y + step_x).wait_recv()
            pair_copy(step_x, core).start()
    for half in range(2):
        for step in range(1, chips):
            term_copy(half * chips + step).wait_send()
    for step in range(1, groups):
        turn_copy(step).wait_send()
    for step_x in range(ROW_X):
        pair_copy(step_x, 1 - core).wait_recv()
    halves = jnp.concatenate([coarse_ref[c].reshape(groups * lam_dev, lanes) for c in range(2)], axis=1)
    even = jnp.dot(halves, to_even, preferred_element_type=F32)
    odd = jnp.dot(halves, to_odd, preferred_element_type=F32)
    for pair in range(groups // 2):
        kept = [(number % ROW_X * row_y + number // ROW_X) * lam_dev for number in (2 * pair, 2 * pair + 1)]
        first = even[kept[0] : kept[0] + lam_dev]
        second = odd[kept[1] : kept[1] + lam_dev]
        base = pair * 3 * lanes
        ordered_ref[:, base : base + lanes] = first[:, :lanes]
        ordered_ref[:, base + lanes : base + 2 * lanes] = first[:, lanes:] + second[:, :lanes]
        ordered_ref[:, base + 2 * lanes : base + 3 * lanes] = second[:, lanes:]

    for step_x in range(ROW_X):
        pair_copy(step_x, core).wait_send()
    for step in range(1, parts):
        dual_copy(step).wait_send()
    for step in range(1, parts):
        dual_arrival(step).wait_recv()
    for entry in range(refined_ref.shape[1]):
        blocks_ref[entry] = dual_ref[lax.shift_right_logical(refined_ref[0, entry], slots - 1)]


def write_out(blocks_ref, ordered_ref, blocks_out, ordered_out, sem):
    copies = []
    for number, (source, target) in enumerate(((blocks_ref, blocks_out), (ordered_ref, ordered_out))):
        half = source.shape[0] // 2
        for at in range(2):
            rows = pl.ds(at * half, half)
            copies.append(pltpu.make_async_copy(source.at[rows], target.at[rows], sem.at[2 * number + at]))
    for copy in copies:
        copy.start()
    for copy in copies:
        copy.wait()


def on_device(groups, parts, factor_inv, b_rows, b_coef, b_count, refined, modes, owner, lam_dev):
    slots, order, _ = factor_inv.shape
    width = b_rows.shape[1]
    mode_count = modes.shape[1]
    share = width // parts
    chips = parts // 2
    rows = slots * SLOT_ROWS
    lanes = chips * rows
    lam = groups * lam_dev
    columns = groups * parts * slots * mode_count
    vmem = pl.BlockSpec(memory_space=pltpu.VMEM)
    anywhere = pl.BlockSpec(memory_space=pl.ANY)
    inputs = (b_count, refined, b_rows, b_coef, jnp.transpose(modes, (1, 0, 2)), owner, factor_inv)
    blocks, ordered = pl.pallas_call(
        functools.partial(assemble_and_send, groups, parts, lam_dev),
        out_shape=(
            pltpu.VMEM((refined.shape[1], share, width), BF16),
            pltpu.VMEM((lam_dev, columns), F32),
        ),
        in_specs=[anywhere] * 7,
        out_specs=(vmem, vmem),
        scratch_shapes=[
            pltpu.SMEM(b_count.shape, jnp.int32),
            pltpu.SMEM(refined.shape, jnp.int32),
            pltpu.VMEM(b_rows.shape, jnp.int32),
            pltpu.VMEM(b_coef.shape, F32),
            pltpu.VMEM((mode_count, slots, order), F32),
            pltpu.VMEM(owner.shape, jnp.int32),
            [pltpu.VMEM((slots, X_TILE, order), BF16) for _ in range(order // X_TILE)],
            pltpu.VMEM((order, width), BF16),
            pltpu.VMEM((slots, 1, width), F32),
            pltpu.VMEM((rows, order), F32),
            pltpu.VMEM((order, width), BF16),
            pltpu.VMEM((width, width), BF16),
            pltpu.VMEM((rows, lam), BF16),
            pltpu.VMEM((chips, rows, lam), BF16),
            pltpu.VMEM((lam, lanes), BF16),
            pltpu.VMEM((2, groups, lam_dev, lanes), BF16),
            pltpu.VMEM((parts, share, width), BF16),
            pltpu.SemaphoreType.DMA((6,)),
            pltpu.SemaphoreType.DMA((order // X_TILE,)),
            pltpu.SemaphoreType.DMA((parts,)),
            pltpu.SemaphoreType.DMA((parts,)),
            pltpu.SemaphoreType.DMA((2 * chips,)),
            pltpu.SemaphoreType.DMA((2 * chips,)),
            pltpu.SemaphoreType.DMA((groups,)),
            pltpu.SemaphoreType.DMA((groups,)),
            pltpu.SemaphoreType.DMA((ROW_X,)),
            pltpu.SemaphoreType.DMA((ROW_X,)),
            pltpu.SemaphoreType.REGULAR,
        ],
        compiler_params=pltpu.CompilerParams(
            collective_id=0, has_side_effects=True, vmem_limit_bytes=VMEM_LIMIT
        ),
        name="assemble_and_send",
    )(*(pltpu.with_memory_space_constraint(array, pltpu.HBM) for array in inputs))
    blocks, ordered = pl.pallas_call(
        write_out,
        out_shape=(
            jax.ShapeDtypeStruct(blocks.shape, BF16),
            jax.ShapeDtypeStruct(ordered.shape, F32),
        ),
        in_specs=[vmem, vmem],
        out_specs=(anywhere, anywhere),
        scratch_shapes=[pltpu.SemaphoreType.DMA((4,))],
        compiler_params=pltpu.CompilerParams(vmem_limit_bytes=2 * 1024 * 1024),
        name="write_out",
    )(*(pltpu.with_memory_space_constraint(array, pltpu.VMEM) for array in (blocks, ordered)))
    return blocks, ordered.T


def solution(mesh):
    groups, parts = mesh.shape["row"], mesh.shape["help"]
    lam_dev = 16
    in_specs = (
        P(("row", "help"), None, None),
        P(("row", "help"), None),
        P(("row", "help"), None),
        P(("row", "help")),
        P("row", None),
        P(("row", "help"), None, None),
        P(("row", "help"), None),
    )
    out_specs = (P("row", "help", None), P(None, "row"))

    def body(*args):
        return on_device(groups, parts, *args, lam_dev)

    return jax.shard_map(body, mesh=mesh, in_specs=in_specs, out_specs=out_specs, check_vma=False)
```

```python
import functools

import jax
import jax.numpy as jnp
from jax import lax
from jax.experimental import pallas as pl
from jax.experimental.pallas import tpu as pltpu
from jax.sharding import PartitionSpec as P

MESH = pl.DeviceIdType.MESH
BF16 = jnp.bfloat16
F32 = jnp.float32
SLOT_ROWS = 8
LANES = 128
X_TILE = 256
GRAM_TILE = 256
FIRST_CHIPS = 1
VMEM_LIMIT = 28 * 1024 * 1024
ROW_X = 4


def one_hot(rows, count):
    at = lax.broadcasted_iota(jnp.int32, (count, rows.shape[1]), 0)
    return jnp.where(at == rows, F32(1.0), F32(0.0)).astype(BF16)


def two_parts(x):
    high = x.astype(BF16)
    low = (x - high.astype(F32)).astype(BF16)
    return jnp.concatenate([high, low], axis=0)


def sum_parts(x):
    half = x.shape[0] // 2
    return x[:half] + x[half:]


def ring_distance(step, size):
    return min(step, size - step)


def far_first(steps, sizes):
    def way(step):
        return -sum(ring_distance(a, n) for a, n in zip(step, sizes))
    return sorted((step for step in steps if any(step)), key=way)


def owner_place(owner, x, lam_dev, column_share):
    shift = lam_dev.bit_length() - 1
    holder = lax.shift_right_logical(owner, shift)
    place = lax.bitwise_and(x + 2 - lax.bitwise_and(holder, ROW_X - 1), ROW_X - 1)
    holder_y = lax.shift_right_logical(holder, ROW_X.bit_length() - 1)
    return place * column_share + holder_y * lam_dev + lax.bitwise_and(owner, lam_dev - 1)


def pick_lanes(table, rows):
    height, order = table.shape
    pieces = []
    for piece in range(rows.shape[1] // LANES):
        index = jnp.broadcast_to(rows[:, piece * LANES : (piece + 1) * LANES], (height, LANES))
        block, lane = lax.shift_right_logical(index, 7), lax.bitwise_and(index, LANES - 1)
        found = jnp.zeros((height, LANES), table.dtype)
        for source in range(order // LANES):
            values = jnp.take_along_axis(
                table[:, source * LANES : (source + 1) * LANES], lane, axis=1, mode="promise_in_bounds"
            )
            found = jnp.where(block == source, values, found)
        pieces.append(found)
    return jnp.concatenate(pieces, axis=1)


def assemble_and_send(
    groups, parts, lam_dev,
    count_hbm, refined_hbm, rows_hbm, coef_hbm, modes_hbm, owner_hbm, factor_hbm,
    blocks_ref, ordered_ref,
    count_ref, refined_ref, rows_ref, coef_ref, modes_ref, owner_ref,
    factor, picker, weight, stacked, panel, gram, term, terms, turned, coarse_ref, dual_ref,
    small_sem, load_sem, send_dual, recv_dual, send_term, recv_term, send_turn, recv_turn, send_pair, recv_pair, row_ready,
):
    row = lax.axis_index("row")
    part = lax.axis_index("help")
    core = lax.rem(part, 2)
    chip = lax.div(part, 2)
    chips = parts // 2
    slots, order, _ = factor_hbm.shape
    width = rows_ref.shape[1]
    modes = modes_ref.shape[0]
    lam = groups * lam_dev
    share = width // parts
    y, x = lax.div(row, ROW_X), lax.rem(row, ROW_X)
    row_y = groups // ROW_X
    chip_ahead = [lax.rem(chip + step, chips) for step in range(chips)]
    chip_behind = [lax.rem(chip + chips - step, chips) for step in range(chips)]
    core_at = [core, 1 - core]
    y_ahead = [lax.rem(y + step, row_y) for step in range(row_y)]
    y_behind = [lax.rem(y + row_y - step, row_y) for step in range(row_y)]
    x_ahead = [lax.rem(x + step, ROW_X) for step in range(ROW_X)]
    x_behind = [lax.rem(x + ROW_X - step, ROW_X) for step in range(ROW_X)]
    column_share = row_y * lam_dev
    half_width = lam // 2

    small = [
        pltpu.make_async_copy(source, target, small_sem.at[number])
        for number, (source, target) in enumerate((
            (rows_hbm, rows_ref), (owner_hbm, owner_ref), (modes_hbm, modes_ref), (coef_hbm, coef_ref),
            (count_hbm, count_ref), (refined_hbm, refined_ref),
        ))
    ]
    for copy in small:
        copy.start()
    loads = []
    for tile in range(order // X_TILE):
        at = pl.ds(tile * X_TILE, X_TILE)
        loads.append(pltpu.make_async_copy(factor_hbm.at[:, at, :], factor[tile], load_sem.at[tile]))
        loads[-1].start()

    barrier = pltpu.get_barrier_semaphore()

    def greet_help(step, _):
        pl.semaphore_signal(barrier, inc=1, device_id=(row, lax.rem(part + step, parts)), device_id_type=MESH)
        return 0

    head = groups // 2

    @pl.when(row != head)
    def _():
        pl.semaphore_signal(barrier, inc=1, device_id=(head, part), device_id_type=MESH)

    lax.fori_loop(1, parts, greet_help, 0)

    stacked[...] = jnp.zeros_like(stacked)
    column = lax.broadcasted_iota(jnp.int32, (1, width), 1)
    for copy in small:
        copy.wait()
    for slot in range(slots):
        stacked[slot * SLOT_ROWS : slot * SLOT_ROWS + modes, :] = modes_ref[:, slot, :]
        weight[slot] = jnp.where(column < count_ref[slot], coef_ref[slot : slot + 1, :], F32(0.0))
    totals = []
    for slot in range(slots):
        table = stacked[slot * SLOT_ROWS : (slot + 1) * SLOT_ROWS, :]
        values = pick_lanes(table, rows_ref[slot : slot + 1, :]) * weight[slot]
        owned = one_hot(owner_place(owner_ref[slot : slot + 1, :], x, lam_dev, column_share), lam)
        totals.append(sum_parts(
            lax.dot_general(two_parts(values), owned, (((1,), (1,)), ((), ())), preferred_element_type=F32)
        ))
    total = jnp.concatenate(totals, axis=0).astype(BF16)
    term[...] = total
    terms[chip] = total

    def term_copy_to(other, half):
        step = lax.rem(other + chips - chip, chips) + half * chips
        at = pl.ds(half * half_width, half_width)
        return pltpu.make_async_remote_copy(
            src_ref=term.at[:, at], dst_ref=terms.at[chip, :, at],
            send_sem=send_term.at[step], recv_sem=recv_term.at[step],
            device_id=(row, other * 2 + core), device_id_type=MESH,
        )

    def term_copy(step):
        return term_copy_to(chip_ahead[step % chips], step // chips)

    def term_arrival(step):
        other = chip_behind[step % chips]
        at = pl.ds(step // chips * half_width, half_width)
        return pltpu.make_async_remote_copy(
            src_ref=term.at[:, at], dst_ref=terms.at[other, :, at],
            send_sem=send_term.at[step], recv_sem=recv_term.at[step],
            device_id=(row, other * 2 + core), device_id_type=MESH,
        )

    def row_is_here(step, _):
        pl.semaphore_signal(row_ready, inc=1, device_id=(lax.rem(row + step, groups), part), device_id_type=MESH)
        return 0

    def meet_and_send_terms():
        pl.semaphore_wait(barrier, parts - 1 + jnp.where(row == head, groups - 1, 0))

        @pl.when(row == head)
        def _():
            lax.fori_loop(1, groups, row_is_here, 0)

        for half in range(2):
            for other in range(chips):
                @pl.when(other != chip)
                def _(other=other, half=half):
                    term_copy_to(other, half).start()

    late = chip >= chips // 2

    @pl.when(late)
    def _():
        meet_and_send_terms()

    chosen = jnp.int32(0)
    for entry in range(refined_ref.shape[1]):
        listed = refined_ref[0, entry]
        chosen = jnp.where(listed == part * slots + 1, jnp.int32(1), chosen)
    rows_here = jnp.where(chosen == 1, rows_ref[1:2, :], rows_ref[0:1, :])
    picker[...] = one_hot(rows_here, order)
    scale = weight[chosen]
    for tile in range(order // X_TILE):
        loads[tile].wait()
        picked = jnp.dot(factor[tile][chosen], picker[...], preferred_element_type=F32)
        panel[pl.ds(tile * X_TILE, X_TILE), :] = (picked * scale).astype(BF16)
    for tile in range(width // GRAM_TILE):
        at = pl.ds(tile * GRAM_TILE, GRAM_TILE)
        gram[at, :] = lax.dot_general(
            panel[:, at], panel[...], (((0,), (0,)), ((), ())), preferred_element_type=F32
        ).astype(BF16)

    def dual_copy_to(other_chip, other_core):
        step = lax.rem(other_chip + chips - chip, chips) * 2 + other_core
        other = other_chip * 2 + core_at[other_core]
        return pltpu.make_async_remote_copy(
            src_ref=gram.at[pl.ds(other * share, share), :], dst_ref=dual_ref.at[part],
            send_sem=send_dual.at[step], recv_sem=recv_dual.at[step],
            device_id=(row, other), device_id_type=MESH,
        )

    def dual_copy(step):
        return dual_copy_to(chip_ahead[step // 2], step % 2)

    def dual_arrival(step):
        other = chip_behind[step // 2] * 2 + core_at[step % 2]
        return pltpu.make_async_remote_copy(
            src_ref=gram.at[pl.ds(other * share, share), :], dst_ref=dual_ref.at[other],
            send_sem=send_dual.at[step], recv_sem=recv_dual.at[step],
            device_id=(row, other), device_id_type=MESH,
        )

    @pl.when(jnp.logical_not(late))
    def _():
        meet_and_send_terms()

    for other_chip in range(FIRST_CHIPS):
        @pl.when(other_chip != chip)
        def _(other_chip=other_chip):
            for other_core in range(2):
                dual_copy_to(other_chip, other_core).start()

    for z, other_core in far_first([(z, c) for z in range(chips) for c in range(2)], (chips, 2)):
        if z == 0:
            dual_copy(other_core).start()
            continue

        @pl.when(chip_ahead[z] >= FIRST_CHIPS)
        def _(z=z, other_core=other_core):
            dual_copy(2 * z + other_core).start()
    dual_ref[part] = gram[pl.ds(part * share, share), :]

    lanes = chips * slots * SLOT_ROWS

    def turn_copy(step):
        other_y, other_x = y_ahead[step // ROW_X], x_ahead[step % ROW_X]
        start_row = (ROW_X + 2 - step % ROW_X) % ROW_X * column_share + other_y * lam_dev
        return pltpu.make_async_remote_copy(
            src_ref=turned.at[pl.ds(pl.multiple_of(start_row, lam_dev), lam_dev), :],
            dst_ref=coarse_ref.at[core, x * row_y + y],
            send_sem=send_turn.at[step], recv_sem=recv_turn.at[step],
            device_id=(other_y * ROW_X + other_x, part), device_id_type=MESH,
        )

    def turn_arrival(step):
        other_y, other_x = y_behind[step // ROW_X], x_behind[step % ROW_X]
        return pltpu.make_async_remote_copy(
            src_ref=turned.at[pl.ds(0, lam_dev), :], dst_ref=coarse_ref.at[core, other_x * row_y + other_y],
            send_sem=send_turn.at[step], recv_sem=recv_turn.at[step],
            device_id=(other_y * ROW_X + other_x, part), device_id_type=MESH,
        )

    @pl.when(row != head)
    def _():
        pl.semaphore_wait(row_ready, 1)

    halves_of_x = ((2, 1), (0, 3))
    for half, steps_x in enumerate(halves_of_x):
        for step in range(1, chips):
            term_arrival(half * chips + step).wait_recv()
        at = slice(half * half_width, (half + 1) * half_width)
        beside = terms[:, :, at].reshape(lanes, half_width)
        turned[at, :] = jnp.transpose(beside.astype(F32)).astype(BF16)
        for step_y, step_x in far_first([(a, b) for a in range(row_y) for b in steps_x], (row_y, ROW_X)):
            turn_copy(ROW_X * step_y + step_x).start()
    coarse_ref[core, x * row_y + y] = turned[pl.ds(2 * column_share + y * lam_dev, lam_dev), :]

    source = lax.broadcasted_iota(jnp.int32, (2 * lanes, 1), 0)
    from_core, inside = source // lanes, source % lanes
    from_chip, at = inside // (slots * SLOT_ROWS), inside % (slots * SLOT_ROWS)
    from_slot, mode = at // SLOT_ROWS, at % SLOT_ROWS
    target = jnp.where(mode < modes, ((from_chip * 2 + from_core) * slots + from_slot) * modes + mode, -512)
    lane = lax.broadcasted_iota(jnp.int32, (2 * lanes, 2 * lanes), 1)
    shift = parts * slots * modes - lanes
    to_even = jnp.where(lane == target, F32(1.0), F32(0.0)).astype(BF16)
    to_odd = jnp.where(lane == target + shift, F32(1.0), F32(0.0)).astype(BF16)

    there = chip * 2 + 1 - core

    def pair_copy(step_x, half):
        at = pl.ds(x_behind[step_x] * row_y, row_y)
        return pltpu.make_async_remote_copy(
            src_ref=coarse_ref.at[half, at], dst_ref=coarse_ref.at[half, at],
            send_sem=send_pair.at[step_x], recv_sem=recv_pair.at[step_x],
            device_id=(row, there), device_id_type=MESH,
        )

    for steps_x in halves_of_x:
        for step_x in steps_x:
            for step_y in range(row_y):
                if step_y or step_x:
                    turn_arrival(ROW_X * step_y + step_x).wait_recv()
            pair_copy(step_x, core).start()
    for half in range(2):
        for step in range(1, chips):
            term_copy(half * chips + step).wait_send()
    for step in range(1, groups):
        turn_copy(step).wait_send()
    for step_x in range(ROW_X):
        pair_copy(step_x, 1 - core).wait_recv()
    halves = jnp.concatenate([coarse_ref[c].reshape(groups * lam_dev, lanes) for c in range(2)], axis=1)
    even = jnp.dot(halves, to_even, preferred_element_type=F32)
    odd = jnp.dot(halves, to_odd, preferred_element_type=F32)
    for pair in range(groups // 2):
        kept = [(number % ROW_X * row_y + number // ROW_X) * lam_dev for number in (2 * pair, 2 * pair + 1)]
        first = even[kept[0] : kept[0] + lam_dev]
        second = odd[kept[1] : kept[1] + lam_dev]
        base = pair * 3 * lanes
        ordered_ref[:, base : base + lanes] = first[:, :lanes]
        ordered_ref[:, base + lanes : base + 2 * lanes] = first[:, lanes:] + second[:, :lanes]
        ordered_ref[:, base + 2 * lanes : base + 3 * lanes] = second[:, lanes:]

    for step_x in range(ROW_X):
        pair_copy(step_x, core).wait_send()
    for step in range(1, parts):
        dual_copy(step).wait_send()
    for step in range(1, parts):
        dual_arrival(step).wait_recv()
    for entry in range(refined_ref.shape[1]):
        blocks_ref[entry] = dual_ref[lax.shift_right_logical(refined_ref[0, entry], slots - 1)]


def write_out(blocks_ref, ordered_ref, blocks_out, ordered_out, sem):
    copies = []
    for number, (source, target) in enumerate(((blocks_ref, blocks_out), (ordered_ref, ordered_out))):
        half = source.shape[0] // 2
        for at in range(2):
            rows = pl.ds(at * half, half)
            copies.append(pltpu.make_async_copy(source.at[rows], target.at[rows], sem.at[2 * number + at]))
    for copy in copies:
        copy.start()
    for copy in copies:
        copy.wait()


def on_device(groups, parts, factor_inv, b_rows, b_coef, b_count, refined, modes, owner, lam_dev):
    slots, order, _ = factor_inv.shape
    width = b_rows.shape[1]
    mode_count = modes.shape[1]
    share = width // parts
    chips = parts // 2
    rows = slots * SLOT_ROWS
    lanes = chips * rows
    lam = groups * lam_dev
    columns = groups * parts * slots * mode_count
    vmem = pl.BlockSpec(memory_space=pltpu.VMEM)
    anywhere = pl.BlockSpec(memory_space=pl.ANY)
    inputs = (b_count, refined, b_rows, b_coef, jnp.transpose(modes, (1, 0, 2)), owner, factor_inv)
    blocks, ordered = pl.pallas_call(
        functools.partial(assemble_and_send, groups, parts, lam_dev),
        out_shape=(
            pltpu.VMEM((refined.shape[1], share, width), BF16),
            pltpu.VMEM((lam_dev, columns), F32),
        ),
        in_specs=[anywhere] * 7,
        out_specs=(vmem, vmem),
        scratch_shapes=[
            pltpu.SMEM(b_count.shape, jnp.int32),
            pltpu.SMEM(refined.shape, jnp.int32),
            pltpu.VMEM(b_rows.shape, jnp.int32),
            pltpu.VMEM(b_coef.shape, F32),
            pltpu.VMEM((mode_count, slots, order), F32),
            pltpu.VMEM(owner.shape, jnp.int32),
            [pltpu.VMEM((slots, X_TILE, order), BF16) for _ in range(order // X_TILE)],
            pltpu.VMEM((order, width), BF16),
            pltpu.VMEM((slots, 1, width), F32),
            pltpu.VMEM((rows, order), F32),
            pltpu.VMEM((order, width), BF16),
            pltpu.VMEM((width, width), BF16),
            pltpu.VMEM((rows, lam), BF16),
            pltpu.VMEM((chips, rows, lam), BF16),
            pltpu.VMEM((lam, lanes), BF16),
            pltpu.VMEM((2, groups, lam_dev, lanes), BF16),
            pltpu.VMEM((parts, share, width), BF16),
            pltpu.SemaphoreType.DMA((6,)),
            pltpu.SemaphoreType.DMA((order // X_TILE,)),
            pltpu.SemaphoreType.DMA((parts,)),
            pltpu.SemaphoreType.DMA((parts,)),
            pltpu.SemaphoreType.DMA((2 * chips,)),
            pltpu.SemaphoreType.DMA((2 * chips,)),
            pltpu.SemaphoreType.DMA((groups,)),
            pltpu.SemaphoreType.DMA((groups,)),
            pltpu.SemaphoreType.DMA((ROW_X,)),
            pltpu.SemaphoreType.DMA((ROW_X,)),
            pltpu.SemaphoreType.REGULAR,
        ],
        compiler_params=pltpu.CompilerParams(
            collective_id=0, has_side_effects=True, vmem_limit_bytes=VMEM_LIMIT
        ),
        name="assemble_and_send",
    )(*(pltpu.with_memory_space_constraint(array, pltpu.HBM) for array in inputs))
    blocks, ordered = pl.pallas_call(
        write_out,
        out_shape=(
            jax.ShapeDtypeStruct(blocks.shape, BF16),
            jax.ShapeDtypeStruct(ordered.shape, F32),
        ),
        in_specs=[vmem, vmem],
        out_specs=(anywhere, anywhere),
        scratch_shapes=[pltpu.SemaphoreType.DMA((4,))],
        compiler_params=pltpu.CompilerParams(vmem_limit_bytes=2 * 1024 * 1024),
        name="write_out",
    )(*(pltpu.with_memory_space_constraint(array, pltpu.VMEM) for array in (blocks, ordered)))
    return blocks, ordered.T


def solution(mesh):
    groups, parts = mesh.shape["row"], mesh.shape["help"]
    lam_dev = 16
    in_specs = (
        P(("row", "help"), None, None),
        P(("row", "help"), None),
        P(("row", "help"), None),
        P(("row", "help")),
        P("row", None),
        P(("row", "help"), None, None),
        P(("row", "help"), None),
    )
    out_specs = (P("row", "help", None), P(None, "row"))

    def body(*args):
        return on_device(groups, parts, *args, lam_dev)

    return jax.shard_map(body, mesh=mesh, in_specs=in_specs, out_specs=out_specs, check_vma=False)
```

```python
import functools

import jax
import jax.numpy as jnp
from jax import lax
from jax.experimental import pallas as pl
from jax.experimental.pallas import tpu as pltpu
from jax.sharding import PartitionSpec as P

MESH = pl.DeviceIdType.MESH
BF16 = jnp.bfloat16
F32 = jnp.float32
SLOT_ROWS = 8
LANES = 128
X_TILE = 256
GRAM_TILE = 256
FIRST_CHIPS = 1
VMEM_LIMIT = 28 * 1024 * 1024
ROW_X = 4


def one_hot(rows, count):
    at = lax.broadcasted_iota(jnp.int32, (count, rows.shape[1]), 0)
    return jnp.where(at == rows, F32(1.0), F32(0.0)).astype(BF16)


def two_parts(x):
    high = x.astype(BF16)
    low = (x - high.astype(F32)).astype(BF16)
    return jnp.concatenate([high, low], axis=0)


def sum_parts(x):
    half = x.shape[0] // 2
    return x[:half] + x[half:]


def ring_distance(step, size):
    return min(step, size - step)


def far_first(steps, sizes):
    def way(step):
        return -sum(ring_distance(a, n) for a, n in zip(step, sizes))
    return sorted((step for step in steps if any(step)), key=way)


def owner_place(owner, x, lam_dev, column_share):
    shift = lam_dev.bit_length() - 1
    holder = lax.shift_right_logical(owner, shift)
    place = lax.bitwise_and(x + 2 - lax.bitwise_and(holder, ROW_X - 1), ROW_X - 1)
    holder_y = lax.shift_right_logical(holder, ROW_X.bit_length() - 1)
    return place * column_share + holder_y * lam_dev + lax.bitwise_and(owner, lam_dev - 1)


def pick_lanes(table, rows):
    height, order = table.shape
    pieces = []
    for piece in range(rows.shape[1] // LANES):
        index = jnp.broadcast_to(rows[:, piece * LANES : (piece + 1) * LANES], (height, LANES))
        block, lane = lax.shift_right_logical(index, 7), lax.bitwise_and(index, LANES - 1)
        found = jnp.zeros((height, LANES), table.dtype)
        for source in range(order // LANES):
            values = jnp.take_along_axis(
                table[:, source * LANES : (source + 1) * LANES], lane, axis=1, mode="promise_in_bounds"
            )
            found = jnp.where(block == source, values, found)
        pieces.append(found)
    return jnp.concatenate(pieces, axis=1)


def assemble_and_send(
    groups, parts, lam_dev,
    count_hbm, refined_hbm, rows_hbm, coef_hbm, modes_hbm, owner_hbm, factor_hbm,
    blocks_ref, ordered_ref,
    count_ref, refined_ref, rows_ref, coef_ref, modes_ref, owner_ref,
    factor, picker, weight, stacked, panel, gram, term, terms, turned, coarse_ref, dual_ref,
    small_sem, load_sem, send_dual, recv_dual, send_term, recv_term, send_turn, recv_turn, send_pair, recv_pair, row_ready,
):
    row = lax.axis_index("row")
    part = lax.axis_index("help")
    core = lax.rem(part, 2)
    chip = lax.div(part, 2)
    chips = parts // 2
    slots, order, _ = factor_hbm.shape
    width = rows_ref.shape[1]
    modes = modes_ref.shape[0]
    lam = groups * lam_dev
    share = width // parts
    y, x = lax.div(row, ROW_X), lax.rem(row, ROW_X)
    row_y = groups // ROW_X
    chip_ahead = [lax.rem(chip + step, chips) for step in range(chips)]
    chip_behind = [lax.rem(chip + chips - step, chips) for step in range(chips)]
    core_at = [core, 1 - core]
    y_ahead = [lax.rem(y + step, row_y) for step in range(row_y)]
    y_behind = [lax.rem(y + row_y - step, row_y) for step in range(row_y)]
    x_ahead = [lax.rem(x + step, ROW_X) for step in range(ROW_X)]
    x_behind = [lax.rem(x + ROW_X - step, ROW_X) for step in range(ROW_X)]
    column_share = row_y * lam_dev
    half_width = lam // 2

    small = [
        pltpu.make_async_copy(source, target, small_sem.at[number])
        for number, (source, target) in enumerate((
            (rows_hbm, rows_ref), (owner_hbm, owner_ref), (modes_hbm, modes_ref), (coef_hbm, coef_ref),
            (count_hbm, count_ref), (refined_hbm, refined_ref),
        ))
    ]
    for copy in small:
        copy.start()
    loads = []
    for tile in range(order // X_TILE):
        at = pl.ds(tile * X_TILE, X_TILE)
        loads.append(pltpu.make_async_copy(factor_hbm.at[:, at, :], factor[tile], load_sem.at[tile]))
        loads[-1].start()

    barrier = pltpu.get_barrier_semaphore()

    def greet_help(step, _):
        pl.semaphore_signal(barrier, inc=1, device_id=(row, lax.rem(part + step, parts)), device_id_type=MESH)
        return 0

    head = groups // 2

    @pl.when(row != head)
    def _():
        pl.semaphore_signal(barrier, inc=1, device_id=(head, part), device_id_type=MESH)

    lax.fori_loop(1, parts, greet_help, 0)

    stacked[...] = jnp.zeros_like(stacked)
    column = lax.broadcasted_iota(jnp.int32, (1, width), 1)
    for copy in small:
        copy.wait()
    for slot in range(slots):
        stacked[slot * SLOT_ROWS : slot * SLOT_ROWS + modes, :] = modes_ref[:, slot, :]
        weight[slot] = jnp.where(column < count_ref[slot], coef_ref[slot : slot + 1, :], F32(0.0))
    totals = []
    for slot in range(slots):
        table = stacked[slot * SLOT_ROWS : (slot + 1) * SLOT_ROWS, :]
        values = pick_lanes(table, rows_ref[slot : slot + 1, :]) * weight[slot]
        owned = one_hot(owner_place(owner_ref[slot : slot + 1, :], x, lam_dev, column_share), lam)
        totals.append(sum_parts(
            lax.dot_general(two_parts(values), owned, (((1,), (1,)), ((), ())), preferred_element_type=F32)
        ))
    total = jnp.concatenate(totals, axis=0).astype(BF16)
    term[...] = total
    terms[chip] = total

    def term_copy_to(other, half):
        step = lax.rem(other + chips - chip, chips) + half * chips
        at = pl.ds(half * half_width, half_width)
        return pltpu.make_async_remote_copy(
            src_ref=term.at[:, at], dst_ref=terms.at[chip, :, at],
            send_sem=send_term.at[step], recv_sem=recv_term.at[step],
            device_id=(row, other * 2 + core), device_id_type=MESH,
        )

    def term_copy(step):
        return term_copy_to(chip_ahead[step % chips], step // chips)

    def term_arrival(step):
        other = chip_behind[step % chips]
        at = pl.ds(step // chips * half_width, half_width)
        return pltpu.make_async_remote_copy(
            src_ref=term.at[:, at], dst_ref=terms.at[other, :, at],
            send_sem=send_term.at[step], recv_sem=recv_term.at[step],
            device_id=(row, other * 2 + core), device_id_type=MESH,
        )

    def row_is_here(step, _):
        pl.semaphore_signal(row_ready, inc=1, device_id=(lax.rem(row + step, groups), part), device_id_type=MESH)
        return 0

    def meet_and_send_terms():
        pl.semaphore_wait(barrier, parts - 1 + jnp.where(row == head, groups - 1, 0))

        @pl.when(row == head)
        def _():
            lax.fori_loop(1, groups, row_is_here, 0)

        for other in range(chips):
            @pl.when(other != chip)
            def _(other=other):
                for half in range(2):
                    term_copy_to(other, half).start()

    late = chip >= chips // 2

    @pl.when(late)
    def _():
        meet_and_send_terms()

    chosen = jnp.int32(0)
    for entry in range(refined_ref.shape[1]):
        listed = refined_ref[0, entry]
        chosen = jnp.where(listed == part * slots + 1, jnp.int32(1), chosen)
    rows_here = jnp.where(chosen == 1, rows_ref[1:2, :], rows_ref[0:1, :])
    picker[...] = one_hot(rows_here, order)
    scale = weight[chosen]
    for tile in range(order // X_TILE):
        loads[tile].wait()
        picked = jnp.dot(factor[tile][chosen], picker[...], preferred_element_type=F32)
        panel[pl.ds(tile * X_TILE, X_TILE), :] = (picked * scale).astype(BF16)
    for tile in range(width // GRAM_TILE):
        at = pl.ds(tile * GRAM_TILE, GRAM_TILE)
        gram[at, :] = lax.dot_general(
            panel[:, at], panel[...], (((0,), (0,)), ((), ())), preferred_element_type=F32
        ).astype(BF16)

    def dual_copy_to(other_chip, other_core):
        step = lax.rem(other_chip + chips - chip, chips) * 2 + other_core
        other = other_chip * 2 + core_at[other_core]
        return pltpu.make_async_remote_copy(
            src_ref=gram.at[pl.ds(other * share, share), :], dst_ref=dual_ref.at[part],
            send_sem=send_dual.at[step], recv_sem=recv_dual.at[step],
            device_id=(row, other), device_id_type=MESH,
        )

    def dual_copy(step):
        return dual_copy_to(chip_ahead[step // 2], step % 2)

    def dual_arrival(step):
        other = chip_behind[step // 2] * 2 + core_at[step % 2]
        return pltpu.make_async_remote_copy(
            src_ref=gram.at[pl.ds(other * share, share), :], dst_ref=dual_ref.at[other],
            send_sem=send_dual.at[step], recv_sem=recv_dual.at[step],
            device_id=(row, other), device_id_type=MESH,
        )

    @pl.when(jnp.logical_not(late))
    def _():
        meet_and_send_terms()

    for other_chip in range(FIRST_CHIPS):
        @pl.when(other_chip != chip)
        def _(other_chip=other_chip):
            for other_core in range(2):
                dual_copy_to(other_chip, other_core).start()

    for z, other_core in far_first([(z, c) for z in range(chips) for c in range(2)], (chips, 2)):
        if z == 0:
            dual_copy(other_core).start()
            continue

        @pl.when(chip_ahead[z] >= FIRST_CHIPS)
        def _(z=z, other_core=other_core):
            dual_copy(2 * z + other_core).start()
    dual_ref[part] = gram[pl.ds(part * share, share), :]

    lanes = chips * slots * SLOT_ROWS

    def turn_copy(step):
        other_y, other_x = y_ahead[step // ROW_X], x_ahead[step % ROW_X]
        start_row = (ROW_X + 2 - step % ROW_X) % ROW_X * column_share + other_y * lam_dev
        return pltpu.make_async_remote_copy(
            src_ref=turned.at[pl.ds(pl.multiple_of(start_row, lam_dev), lam_dev), :],
            dst_ref=coarse_ref.at[core, x * row_y + y],
            send_sem=send_turn.at[step], recv_sem=recv_turn.at[step],
            device_id=(other_y * ROW_X + other_x, part), device_id_type=MESH,
        )

    def turn_arrival(step):
        other_y, other_x = y_behind[step // ROW_X], x_behind[step % ROW_X]
        return pltpu.make_async_remote_copy(
            src_ref=turned.at[pl.ds(0, lam_dev), :], dst_ref=coarse_ref.at[core, other_x * row_y + other_y],
            send_sem=send_turn.at[step], recv_sem=recv_turn.at[step],
            device_id=(other_y * ROW_X + other_x, part), device_id_type=MESH,
        )

    @pl.when(row != head)
    def _():
        pl.semaphore_wait(row_ready, 1)

    halves_of_x = ((2, 1), (0, 3))
    for half, steps_x in enumerate(halves_of_x):
        for step in range(1, chips):
            term_arrival(half * chips + step).wait_recv()
        at = slice(half * half_width, (half + 1) * half_width)
        beside = terms[:, :, at].reshape(lanes, half_width)
        turned[at, :] = jnp.transpose(beside.astype(F32)).astype(BF16)
        for step_y, step_x in far_first([(a, b) for a in range(row_y) for b in steps_x], (row_y, ROW_X)):
            turn_copy(ROW_X * step_y + step_x).start()
    coarse_ref[core, x * row_y + y] = turned[pl.ds(2 * column_share + y * lam_dev, lam_dev), :]

    source = lax.broadcasted_iota(jnp.int32, (2 * lanes, 1), 0)
    from_core, inside = source // lanes, source % lanes
    from_chip, at = inside // (slots * SLOT_ROWS), inside % (slots * SLOT_ROWS)
    from_slot, mode = at // SLOT_ROWS, at % SLOT_ROWS
    target = jnp.where(mode < modes, ((from_chip * 2 + from_core) * slots + from_slot) * modes + mode, -512)
    lane = lax.broadcasted_iota(jnp.int32, (2 * lanes, 2 * lanes), 1)
    shift = parts * slots * modes - lanes
    to_even = jnp.where(lane == target, F32(1.0), F32(0.0)).astype(BF16)
    to_odd = jnp.where(lane == target + shift, F32(1.0), F32(0.0)).astype(BF16)

    there = chip * 2 + 1 - core

    def pair_copy(step_x, half):
        at = pl.ds(x_behind[step_x] * row_y, row_y)
        return pltpu.make_async_remote_copy(
            src_ref=coarse_ref.at[half, at], dst_ref=coarse_ref.at[half, at],
            send_sem=send_pair.at[step_x], recv_sem=recv_pair.at[step_x],
            device_id=(row, there), device_id_type=MESH,
        )

    for steps_x in halves_of_x:
        for step_x in steps_x:
            for step_y in range(row_y):
                if step_y or step_x:
                    turn_arrival(ROW_X * step_y + step_x).wait_recv()
            pair_copy(step_x, core).start()
    for half in range(2):
        for step in range(1, chips):
            term_copy(half * chips + step).wait_send()
    for step in range(1, groups):
        turn_copy(step).wait_send()
    for step_x in range(ROW_X):
        pair_copy(step_x, 1 - core).wait_recv()
    halves = jnp.concatenate([coarse_ref[c].reshape(groups * lam_dev, lanes) for c in range(2)], axis=1)
    even = jnp.dot(halves, to_even, preferred_element_type=F32)
    odd = jnp.dot(halves, to_odd, preferred_element_type=F32)
    for pair in range(groups // 2):
        kept = [(number % ROW_X * row_y + number // ROW_X) * lam_dev for number in (2 * pair, 2 * pair + 1)]
        first = even[kept[0] : kept[0] + lam_dev]
        second = odd[kept[1] : kept[1] + lam_dev]
        base = pair * 3 * lanes
        ordered_ref[:, base : base + lanes] = first[:, :lanes]
        ordered_ref[:, base + lanes : base + 2 * lanes] = first[:, lanes:] + second[:, :lanes]
        ordered_ref[:, base + 2 * lanes : base + 3 * lanes] = second[:, lanes:]

    for step_x in range(ROW_X):
        pair_copy(step_x, core).wait_send()
    for step in range(1, parts):
        dual_copy(step).wait_send()
    for step in range(1, parts):
        dual_arrival(step).wait_recv()
    for entry in range(refined_ref.shape[1]):
        blocks_ref[entry] = dual_ref[lax.shift_right_logical(refined_ref[0, entry], slots - 1)]


def write_out(blocks_ref, ordered_ref, blocks_out, ordered_out, sem):
    copies = []
    for number, (source, target) in enumerate(((blocks_ref, blocks_out), (ordered_ref, ordered_out))):
        half = source.shape[0] // 2
        for at in range(2):
            rows = pl.ds(at * half, half)
            copies.append(pltpu.make_async_copy(source.at[rows], target.at[rows], sem.at[2 * number + at]))
    for copy in copies:
        copy.start()
    for copy in copies:
        copy.wait()


def on_device(groups, parts, factor_inv, b_rows, b_coef, b_count, refined, modes, owner, lam_dev):
    slots, order, _ = factor_inv.shape
    width = b_rows.shape[1]
    mode_count = modes.shape[1]
    share = width // parts
    chips = parts // 2
    rows = slots * SLOT_ROWS
    lanes = chips * rows
    lam = groups * lam_dev
    columns = groups * parts * slots * mode_count
    vmem = pl.BlockSpec(memory_space=pltpu.VMEM)
    anywhere = pl.BlockSpec(memory_space=pl.ANY)
    inputs = (b_count, refined, b_rows, b_coef, jnp.transpose(modes, (1, 0, 2)), owner, factor_inv)
    blocks, ordered = pl.pallas_call(
        functools.partial(assemble_and_send, groups, parts, lam_dev),
        out_shape=(
            pltpu.VMEM((refined.shape[1], share, width), BF16),
            pltpu.VMEM((lam_dev, columns), F32),
        ),
        in_specs=[anywhere] * 7,
        out_specs=(vmem, vmem),
        scratch_shapes=[
            pltpu.SMEM(b_count.shape, jnp.int32),
            pltpu.SMEM(refined.shape, jnp.int32),
            pltpu.VMEM(b_rows.shape, jnp.int32),
            pltpu.VMEM(b_coef.shape, F32),
            pltpu.VMEM((mode_count, slots, order), F32),
            pltpu.VMEM(owner.shape, jnp.int32),
            [pltpu.VMEM((slots, X_TILE, order), BF16) for _ in range(order // X_TILE)],
            pltpu.VMEM((order, width), BF16),
            pltpu.VMEM((slots, 1, width), F32),
            pltpu.VMEM((rows, order), F32),
            pltpu.VMEM((order, width), BF16),
            pltpu.VMEM((width, width), BF16),
            pltpu.VMEM((rows, lam), BF16),
            pltpu.VMEM((chips, rows, lam), BF16),
            pltpu.VMEM((lam, lanes), BF16),
            pltpu.VMEM((2, groups, lam_dev, lanes), BF16),
            pltpu.VMEM((parts, share, width), BF16),
            pltpu.SemaphoreType.DMA((6,)),
            pltpu.SemaphoreType.DMA((order // X_TILE,)),
            pltpu.SemaphoreType.DMA((parts,)),
            pltpu.SemaphoreType.DMA((parts,)),
            pltpu.SemaphoreType.DMA((2 * chips,)),
            pltpu.SemaphoreType.DMA((2 * chips,)),
            pltpu.SemaphoreType.DMA((groups,)),
            pltpu.SemaphoreType.DMA((groups,)),
            pltpu.SemaphoreType.DMA((ROW_X,)),
            pltpu.SemaphoreType.DMA((ROW_X,)),
            pltpu.SemaphoreType.REGULAR,
        ],
        compiler_params=pltpu.CompilerParams(
            collective_id=0, has_side_effects=True, vmem_limit_bytes=VMEM_LIMIT
        ),
        name="assemble_and_send",
    )(*(pltpu.with_memory_space_constraint(array, pltpu.HBM) for array in inputs))
    blocks, ordered = pl.pallas_call(
        write_out,
        out_shape=(
            jax.ShapeDtypeStruct(blocks.shape, BF16),
            jax.ShapeDtypeStruct(ordered.shape, F32),
        ),
        in_specs=[vmem, vmem],
        out_specs=(anywhere, anywhere),
        scratch_shapes=[pltpu.SemaphoreType.DMA((4,))],
        compiler_params=pltpu.CompilerParams(vmem_limit_bytes=2 * 1024 * 1024),
        name="write_out",
    )(*(pltpu.with_memory_space_constraint(array, pltpu.VMEM) for array in (blocks, ordered)))
    return blocks, ordered.T


def solution(mesh):
    groups, parts = mesh.shape["row"], mesh.shape["help"]
    lam_dev = 16
    in_specs = (
        P(("row", "help"), None, None),
        P(("row", "help"), None),
        P(("row", "help"), None),
        P(("row", "help")),
        P("row", None),
        P(("row", "help"), None, None),
        P(("row", "help"), None),
    )
    out_specs = (P("row", "help", None), P(None, "row"))

    def body(*args):
        return on_device(groups, parts, *args, lam_dev)

    return jax.shard_map(body, mesh=mesh, in_specs=in_specs, out_specs=out_specs, check_vma=False)
```
